128 devices in a mesh: group: 4 (over y_lo, core), region: 32 (over x, z, y_hi).
Axes of the slice: x: 4, y: 4 (y_hi: 2, y_lo: 2; y = y_hi * 2 + y_lo), z: 4, core: 2. Of those that a mesh axis runs over, the one named last changes fastest.
Arguments:
- object_field: float32 [2, 16384, 2048], P(None, 'region', 'group'), may hold values from -6 to 6
- probe: float32 [2, 4, 256, 256], replicated, may hold values from -2 to 2
- amplitudes: float32 [128, 1024, 256], P('region', 'group'), may hold values from 0.25 to 4
- positions: int32 [128, 8], P('region', 'group'), may hold values from 0 to 256
- dual_top: float32 [2, 2048, 2048], P(None, 'region', 'group'), may hold values from -1.75 to 1.75
- dual_bottom: float32 [2, 2048, 2048], P(None, 'region', 'group'), may hold values from -1.75 to 1.75
- pieces: int32 [64, 4], P('region', 'group'), may hold values from 0 to 3, as said below
- live: int32 [32, 4], P('region', 'group'), may hold values from 1 to 2
Outputs:
- object_new: float32 [2, 16384, 2048], P(None, 'region', 'group')
- probe_new: float32 [2, 4, 256, 256], replicated
- dual_top_new: float32 [2, 2048, 2048], P(None, 'region', 'group')
- dual_bottom_new: float32 [2, 2048, 2048], P(None, 'region', 'group')
The draws below stay inside these ranges and needn't reach their ends.
Inputs may be any that keep to these rules, and one draw needn't show every extreme that they name: `pieces`: within one tile the 2 listed blocks are distinct.
All inputs are finite; a program needn't handle non-finite values.
Results may differ from the reference program's by a relative error of at most 0.0001.
Values sent between devices are 32-bit elements; how exact they have to be, the bound alone decides.
A program may use at most 128 MiB of HBM per device.

```python
import math
import jax
import jax.numpy as jnp
from jax import lax

PAT = 256
MODES = 4
NPAT = 4
TILE = 512
EDGE = 64
BLOCK = 128
NPIECE = 4
KP = 2
N_GROUP = 4
N_REGION = 32


def draw_object_field(key, part):
    key = jax.random.fold_in(key, 5)
    rows = jnp.arange(N_REGION * TILE, dtype=jnp.int32) // TILE
    scaling = 0.5 + rows.astype(jnp.float32) / max(N_REGION - 1, 1)
    shape = (2, N_REGION * TILE, N_GROUP * TILE)
    values = jnp.clip(jax.random.normal(key, shape, jnp.float32), -4.0, 4.0) * scaling[None, :, None]
    return values.astype(jnp.float32)


def draw_pieces(key, part):
    key = jax.random.fold_in(key, 11)
    scores = jax.random.randint(key, (N_REGION, N_GROUP, NPIECE), 0, 1 << 20) * NPIECE + jnp.arange(NPIECE, dtype=jnp.int32)
    chosen = jnp.argsort(scores, axis=-1)[..., :KP]
    return chosen.transpose(0, 2, 1).reshape(N_REGION * KP, N_GROUP).astype(jnp.int32)


def draw_live(key, part):
    key = jax.random.fold_in(key, 23)
    first, second = jax.random.split(key)
    counts = jax.random.randint(first, (N_REGION, N_GROUP), 1, KP + 1)
    chosen = jax.random.randint(second, (N_GROUP,), 0, N_REGION)
    filled = jnp.arange(N_REGION, dtype=jnp.int32)[:, None] == chosen[None, :]
    return jnp.where(filled, KP, counts).astype(jnp.int32)


def set_ends(array, key, low, high):
    shape = array.shape
    index_at = [jax.random.randint(jax.random.fold_in(key, axis), (), 0, shape[axis]) for axis in range(len(shape))]
    array = array.at[tuple(index_at)].set(low)
    longest = shape.index(max(shape))
    index_at[longest] = (index_at[longest] + 1) % shape[longest]
    return array.at[tuple(index_at)].set(high)


def levels(stream_key, shape, cuts, low, largest):
    loudness = 1.0
    for axis_at, parts in cuts:
        draws = jax.random.uniform(jax.random.fold_in(jax.random.fold_in(stream_key, 6), axis_at), (parts,), jnp.float32, low / len(cuts), largest / len(cuts))
        loudness = loudness * jnp.repeat(jnp.exp(draws), shape[axis_at] // parts).reshape((-1,) + (1,) * (len(shape) - 1 - axis_at))
    return loudness


def scatter_about(key, dims, width, reach, shards=(), kind=jnp.bfloat16):
    array = width * jax.random.normal(key, dims, jnp.float32)
    if shards:
        array = array * levels(key, dims, shards, -0.22, 0.18)
    return jnp.clip(array, -reach, reach).astype(kind)


def setup_inputs(seed: int = 0) -> dict:
    splits = jax.random.split(jax.random.key(seed), 9)
    object_field = draw_object_field(jax.random.fold_in(splits[8], 71), 0)
    probe = scatter_about(splits[1], (2, MODES, PAT, PAT), 0.35, 2.0, (), jnp.float32)
    amplitudes = jnp.clip(jnp.exp(math.log(4.0) - 2.7725887 * jax.random.uniform(splits[2], (N_REGION * NPAT, N_GROUP * PAT, PAT), jnp.float32) ** levels(splits[2], (N_REGION * NPAT, N_GROUP * PAT, PAT), ((0, 32), (1, 4)), -0.2, 0.2)), 0.25, 4.0)
    positions = set_ends(jax.random.randint(splits[3], (N_REGION * NPAT, N_GROUP * 2), 0, TILE - PAT + 1), jax.random.fold_in(splits[3], 1), 0, TILE - PAT).astype(jnp.int32)
    dual_top = scatter_about(splits[4], (2, N_REGION * EDGE, N_GROUP * TILE), 0.3, 1.75, ((1, 32), (2, 4)), jnp.float32)
    dual_bottom = scatter_about(splits[5], (2, N_REGION * EDGE, N_GROUP * TILE), 0.3, 1.75, ((1, 32), (2, 4)), jnp.float32)
    pieces = draw_pieces(jax.random.fold_in(splits[8], 71), 0)
    live = draw_live(jax.random.fold_in(splits[8], 71), 0)
    return {"object_field": object_field, "probe": probe, "amplitudes": amplitudes, "positions": positions, "dual_top": dual_top, "dual_bottom": dual_bottom, "pieces": pieces, "live": live}


HIGHEST_PRECISION = lax.Precision.HIGHEST

def dft_tables(length):
    counter = jnp.arange(length, dtype=jnp.int32)
    phases = counter[:, None] * counter[None, :] % length
    angles = phases.astype(jnp.float32) * (2.0 * jnp.pi / length)
    scaling = 1.0 / jnp.sqrt(jnp.asarray(length, jnp.float32))
    return (jnp.cos(angles) * scaling, jnp.sin(angles) * scaling)

def apply_left(matrix, field):
    return jnp.einsum('kn,bnm->bkm', matrix, field, precision=HIGHEST_PRECISION)

def apply_right(field, matrix):
    return jnp.einsum('bkn,nm->bkm', field, matrix, precision=HIGHEST_PRECISION)

def transform(real_part, imag_part, cosine_table, sine_table, direction):
    first_real = apply_left(cosine_table, real_part) + direction * apply_left(sine_table, imag_part)
    first_imag = apply_left(cosine_table, imag_part) - direction * apply_left(sine_table, real_part)
    out_real = apply_right(first_real, cosine_table) + direction * apply_right(first_imag, sine_table)
    out_imag = apply_right(first_imag, cosine_table) - direction * apply_right(first_real, sine_table)
    return (out_real, out_imag)

def tile_update(tile_field, scan_rows, measured, probe, cosine_table, sine_table):
    count_scans = scan_rows.shape[0]
    side = probe.shape[2]
    modes = probe.shape[1]
    anchor = jnp.zeros((), jnp.int32)
    patches = jnp.stack([lax.dynamic_slice(tile_field, (anchor, scan_rows[index, 0], scan_rows[index, 1]), (2, side, side)) for index in range(count_scans)])
    patch_real = patches[:, 0][:, None]
    patch_imag = patches[:, 1][:, None]
    probe_real = probe[0][None]
    probe_imag = probe[1][None]
    exit_real = probe_real * patch_real - probe_imag * patch_imag
    exit_imag = probe_real * patch_imag + probe_imag * patch_real
    flat_shape = (count_scans * modes, side, side)
    full_shape = (count_scans, modes, side, side)
    far_real, far_imag = transform(exit_real.reshape(flat_shape), exit_imag.reshape(flat_shape), cosine_table, sine_table, 1.0)
    far_real = far_real.reshape(full_shape)
    far_imag = far_imag.reshape(full_shape)
    modulus = jnp.maximum(jnp.sqrt(lax.optimization_barrier(jnp.sum(far_real * far_real + far_imag * far_imag, axis=1, keepdims=True))), 0.5)
    factor = measured[:, None] / modulus
    back_real, back_imag = transform((far_real * factor).reshape(flat_shape), (far_imag * factor).reshape(flat_shape), cosine_table, sine_table, -1.0)
    change_real = back_real.reshape(full_shape) - exit_real
    change_imag = back_imag.reshape(full_shape) - exit_imag
    grad_real = lax.optimization_barrier(jnp.sum(probe_real * change_real + probe_imag * change_imag, axis=1))
    grad_imag = lax.optimization_barrier(jnp.sum(probe_real * change_imag - probe_imag * change_real, axis=1))
    probe_power = lax.optimization_barrier(jnp.sum(probe[0] * probe[0] + probe[1] * probe[1], axis=0))
    gradient = jnp.zeros(tile_field.shape, jnp.float32)
    weight = jnp.zeros(tile_field.shape[1:], jnp.float32)
    for index in range(count_scans):
        corner = (anchor, scan_rows[index, 0], scan_rows[index, 1])
        window = lax.dynamic_slice(gradient, corner, (2, side, side))
        gradient = lax.dynamic_update_slice(gradient, window + jnp.stack([grad_real[index], grad_imag[index]]), corner)
        corner_flat = (scan_rows[index, 0], scan_rows[index, 1])
        window_flat = lax.dynamic_slice(weight, corner_flat, (side, side))
        weight = lax.dynamic_update_slice(weight, window_flat + probe_power, corner_flat)
    middle = tile_field + gradient / (weight + 1.0)
    numer_real = lax.optimization_barrier(jnp.sum(patch_real * change_real + patch_imag * change_imag, axis=0))
    numer_imag = lax.optimization_barrier(jnp.sum(patch_real * change_imag - patch_imag * change_real, axis=0))
    denom = lax.optimization_barrier(jnp.sum(patches[:, 0] * patches[:, 0] + patches[:, 1] * patches[:, 1], axis=0))
    return (middle, jnp.stack([numer_real, numer_imag]), denom)

def to_tiles(field, rows):
    return field.reshape(2, N_REGION, rows, N_GROUP, TILE).transpose(1, 3, 0, 2, 4)

def from_tiles(tiles, rows):
    return tiles.transpose(2, 0, 3, 1, 4).reshape(2, N_REGION * rows, N_GROUP * TILE)

def reference(object_field, probe, amplitudes, positions, dual_top, dual_bottom, pieces, live):
    cosine_table, sine_table = dft_tables(PAT)
    tiles = to_tiles(object_field, TILE).reshape(N_REGION * N_GROUP, 2, TILE, TILE)
    scans = positions.reshape(N_REGION, NPAT, N_GROUP, 2).transpose(0, 2, 1, 3).reshape(N_REGION * N_GROUP, NPAT, 2)
    measured = amplitudes.reshape(N_REGION, NPAT, N_GROUP, PAT, PAT).transpose(0, 2, 1, 3, 4).reshape(N_REGION * N_GROUP, NPAT, PAT, PAT)

    def step_tile(carry, inputs):
        middle, numer, denom = tile_update(inputs[0], inputs[1], inputs[2], probe, cosine_table, sine_table)
        return ((carry[0] + numer, carry[1] + denom), middle)
    start = (jnp.zeros((2, MODES, PAT, PAT), jnp.float32), jnp.zeros((PAT, PAT), jnp.float32))
    (numer, denom), middles = lax.scan(step_tile, start, (tiles, scans, measured))
    probe_new = probe + numer / (denom + 1.0)
    middles = middles.reshape(N_REGION, N_GROUP, 2, TILE, TILE)
    top_tiles = to_tiles(dual_top, EDGE)
    bottom_tiles = to_tiles(dual_bottom, EDGE)
    listed = pieces.reshape(N_REGION, KP, N_GROUP).transpose(0, 2, 1)
    slot_index = jnp.arange(KP, dtype=jnp.int32)
    usable = slot_index[None, None, :] < live[:, :, None]
    matches = (listed[..., None] == jnp.arange(NPIECE, dtype=jnp.int32)) & usable[..., None]
    covered = jnp.repeat(jnp.any(matches, axis=2), BLOCK, axis=-1)
    edge_mask = covered[:-1, :, None, None, :]
    lower_rows = middles[:-1, :, :, TILE - EDGE:, :]
    upper_rows = middles[1:, :, :, :EDGE, :]
    consensus = 0.5 * (lower_rows + bottom_tiles[:-1] + (upper_rows + top_tiles[1:]))
    bottom_edges = jnp.where(edge_mask, bottom_tiles[:-1] + (lower_rows - consensus), bottom_tiles[:-1])
    top_edges = jnp.where(edge_mask, top_tiles[1:] + (upper_rows - consensus), top_tiles[1:])
    bottom_new = jnp.concatenate([bottom_edges, bottom_tiles[-1:]], axis=0)
    top_new = jnp.concatenate([top_tiles[:1], top_edges], axis=0)
    middles = middles.at[:-1, :, :, TILE - EDGE:, :].set(jnp.where(edge_mask, consensus, lower_rows))
    middles = middles.at[1:, :, :, :EDGE, :].set(jnp.where(edge_mask, consensus, upper_rows))
    return (from_tiles(middles, TILE), probe_new, from_tiles(top_new, EDGE), from_tiles(bottom_new, EDGE))
```

```python
import numpy as np
import jax
import jax.numpy as jnp
import ml_dtypes
from jax import lax
from jax.experimental import pallas as pl
from jax.experimental.pallas import tpu as pltpu
from jax.sharding import PartitionSpec as P

F32, BF16 = jnp.float32, jnp.bfloat16
MESH = pl.DeviceIdType.MESH
PAT, TILE, MODES, NPAT, HALF = 256, 512, 4, 4, 128
EDGE, BLOCK, NPIECE, KP = 64, 128, 4, 2
SUMS = MODES + 1


def tables():
    n = np.arange(HALF)[:, None]
    out = []
    for p in range(2):
        k = 2 * np.arange(HALF)[None, :] + p
        angle = 2 * np.pi * ((n * k) % PAT) / PAT
        c, s = np.cos(angle) / 16.0, np.sin(angle) / 16.0
        full = np.block([[c, -s], [s, c]])
        out.append(full)
    full = np.stack([np.stack(out), np.stack([o.T for o in out])]).astype(np.float32)
    hi = full.astype(ml_dtypes.bfloat16)
    lo = (full - hi.astype(np.float32)).astype(ml_dtypes.bfloat16)
    perm = np.zeros((PAT, PAT), np.float32)
    for j in range(PAT):
        perm[2 * (j % HALF) + j // HALF, j] = 1.0
    return np.stack([hi, lo], axis=2), np.stack([perm, perm.T]).astype(ml_dtypes.bfloat16)


def dot(a, b):
    return jnp.dot(a, b, preferred_element_type=F32)


def split(a):
    h = a.astype(BF16)
    return h, (a - h.astype(F32)).astype(BF16)


def right(a, t, d, p):
    h, l = split(a)
    return dot(h, t[d, p, 0]) + dot(l, t[d, p, 0]) + dot(h, t[d, p, 1])


def left(t, d, p, a):
    h, l = split(a)
    return dot(t[d, p, 0], h) + dot(t[d, p, 1], h) + dot(t[d, p, 0], l)


def along(shape, axis):
    return lax.broadcasted_iota(jnp.int32, shape, axis)


def lane_turn(block, by):
    return pltpu.roll(block, by & (HALF - 1), 1)


def row_turn(block, by):
    return pltpu.roll(block, by & 7, 1)


def window(obj, plane, row, col):
    base = pl.multiple_of(jnp.minimum((row >> 3) << 3, TILE - PAT - 8), 8)
    side = pl.multiple_of(jnp.minimum((col >> 7) << 7, TILE - PAT - HALF), HALF)
    down, right_by = row - base, col - side
    block = obj[plane, pl.ds(base, PAT + 8), pl.ds(side, PAT + HALF)]
    block = block.reshape((PAT + 8) // 8, 8, PAT + HALF)
    turned = row_turn(block, 8 - down)
    keep = along((PAT // 8, 8, PAT + HALF), 1) + down < 8
    block = jnp.where(keep, turned[:-1], turned[1:]).reshape(PAT, PAT + HALF)
    parts = [lane_turn(block[:, t * HALF:(t + 1) * HALF], HALF - right_by) for t in range(3)]
    keep = along((PAT, HALF), 1) + right_by < HALF
    return jnp.concatenate([jnp.where(keep, parts[t], parts[t + 1]) for t in range(2)], axis=1)


def shifted(block, row, col):
    down, right_by = row & 7, col & (HALF - 1)
    keep = along((PAT, HALF), 1) >= right_by
    left_part = lane_turn(block[:, :HALF], right_by)
    right_part = lane_turn(block[:, HALF:], right_by)
    zero = jnp.zeros_like(left_part)
    block = jnp.concatenate([jnp.where(keep, left_part, zero), jnp.where(keep, right_part, left_part), jnp.where(keep, zero, right_part)], axis=1)
    block = row_turn(block.reshape(PAT // 8, 8, PAT + HALF), down)
    edge = jnp.zeros((1, 8, PAT + HALF), F32)
    above = jnp.concatenate([edge, block], axis=0)
    below = jnp.concatenate([block, edge], axis=0)
    keep = along(below.shape, 1) >= down
    return jnp.where(keep, below, above).reshape(PAT + 8, PAT + HALF)


def prepare(pos, pieces, live, obj, probe, patch, inv, columns, rows, mask, gbuf):
    for j in range(NPAT):
        row, col = pos[j, 0], pos[j, 1]
        for plane in range(2):
            patch[j, plane] = window(obj, plane, row, col)
        columns[j] = (along((PAT, TILE), 1) == along((PAT, TILE), 0) + col).astype(F32).astype(BF16)
        rows[:, j * PAT:(j + 1) * PAT] = (along((TILE, PAT), 0) == along((TILE, PAT), 1) + row).astype(F32).astype(BF16)
    gbuf[...] = jnp.zeros_like(gbuf)
    power = sum(probe[0, m] * probe[0, m] + probe[1, m] * probe[1, m] for m in range(MODES))
    weight = jnp.ones((TILE, TILE), F32)
    for j in range(NPAT):
        row, col = pos[j, 0], pos[j, 1]
        gbuf[pl.ds(PAT, PAT + 8), pl.ds(PAT, PAT + HALF)] = shifted(power, row, col)
        top = pl.multiple_of(PAT - ((row >> 3) << 3), 8)
        side = pl.multiple_of(PAT - ((col >> 7) << 7), HALF)
        weight = weight + gbuf[pl.ds(top, TILE), pl.ds(side, TILE)]
    inv[...] = 1.0 / weight
    count, has_lower = live[0, 0], lax.axis_index("region") < 31
    for b in range(NPIECE):
        hit = ((pieces[0, 0] == b) & (count > 0)) | ((pieces[1, 0] == b) & (count > 1))
        value = jnp.where(hit & has_lower, 1.0, 0.0).astype(F32)
        mask[:, b * BLOCK:(b + 1) * BLOCK] = jnp.full((8, BLOCK), value, F32)


class Place:
    def __init__(self):
        group, region = lax.axis_index("group"), lax.axis_index("region")
        self.group, self.region = group, region
        self.core, y_lo = lax.rem(group, 2), group // 2
        self.x, self.z, y_hi = region // 8, lax.rem(region // 2, 4), lax.rem(region, 2)
        self.y = y_hi * 2 + y_lo
        self.plane = self.x * 4 + self.y

    def at(self, x, y, z, core):
        return (lax.rem(y, 2) * 2 + core, (x * 4 + z) * 2 + y // 2)

    def sibling(self):
        return self.at(self.x, self.y, self.z, 1 - self.core)

    def in_plane(self, k):
        x, y = lax.rem(self.x + k // 4, 4), lax.rem(self.y + lax.rem(k, 4), 4)
        return self.at(x, y, self.z, self.core), x * 4 + y

    def on_line(self, k):
        z = lax.rem(self.z + k, 4)
        return self.at(self.x, self.y, z, self.core), z

    def region_by(self, by):
        return (self.group, lax.rem(self.region + 32 + by, 32))


def send(src, dst, sems, index, device):
    copy = pltpu.make_async_remote_copy(
        src_ref=src, dst_ref=dst, send_sem=sems[0].at[index], recv_sem=sems[1].at[index], device_id=device, device_id_type=MESH
    )
    copy.start()


def await_bytes(ref, sem):
    pltpu.make_async_copy(ref, ref, sem).wait()


def kernel(
    patch, inv, columns, place_rows, mask, obj, probe, amp, dual_top, dual_bottom, tab, perm,
    obj_out, probe_out, top_out, bottom_out,
    far, factor, grad, spread_hi, spread_lo, mid, numer,
    from_core, part, from_plane, line, from_line, own, fresh,
    mask_in, up, low, from_below, from_above, top_new, bottom_new,
    core_send, core_recv, plane_send, plane_recv, line_send, line_recv,
    back_line_send, back_line_recv, back_plane_send, back_plane_recv, back_core_send, back_core_recv,
    edge_send, edge_recv, out_sem,
):
    me = Place()
    barrier = pltpu.get_barrier_semaphore()

    def greet(device):
        pl.semaphore_signal(barrier, inc=1, device_id=device, device_id_type=MESH)

    greet(me.sibling())

    def greet_plane(k, _):
        greet(me.in_plane(k)[0])
        return 0

    lax.fori_loop(1, 16, greet_plane, 0)
    for k in range(1, 4):
        greet(me.on_line(k)[0])
    greet(me.region_by(1))
    greet(me.region_by(-1))

    numer[0, MODES] = jnp.zeros((PAT, PAT), F32)
    grad[...] = jnp.zeros_like(grad)

    def forward(j, _):
        pr, pi = patch[j, 0], patch[j, 1]
        numer[0, MODES] += pr * pr + pi * pi

        def mode(m, _):
            pr, pi = patch[j, 0], patch[j, 1]
            qr, qi = probe[0, m], probe[1, m]
            er = qr * pr - qi * pi
            ei = qr * pi + qi * pr
            lo = jnp.concatenate([er[:, :HALF], ei[:, :HALF]], axis=1)
            hi = jnp.concatenate([er[:, HALF:], ei[:, HALF:]], axis=1)
            y0 = right(lo + hi, tab, 0, 0)
            y1 = right(lo - hi, tab, 0, 1)
            yr = jnp.concatenate([y0[:, :HALF], y1[:, :HALF]], axis=1)
            yi = jnp.concatenate([y0[:, HALF:], y1[:, HALF:]], axis=1)
            top = jnp.concatenate([yr[:HALF], yi[:HALF]], axis=0)
            bot = jnp.concatenate([yr[HALF:], yi[HALF:]], axis=0)
            far[m * NPAT + j, 0] = left(tab, 1, 0, top + bot)
            far[m * NPAT + j, 1] = left(tab, 1, 1, top - bot)
            return 0

        lax.fori_loop(0, MODES, mode, 0)
        h, l = split(amp[j])
        h, l = split(dot(h, perm[0]) + dot(l, perm[0]))
        full = dot(perm[1], h) + dot(perm[1], l)
        for q in range(2):
            power = jnp.zeros((HALF, PAT), F32)
            for m in range(MODES):
                z = far[m * NPAT + j, q]
                power = power + z[:HALF] * z[:HALF] + z[HALF:] * z[HALF:]
            f = full[q * HALF:(q + 1) * HALF] / jnp.maximum(jnp.sqrt(power), 0.5)
            factor[j, q, :HALF] = f
            factor[j, q, HALF:] = f
        return 0

    lax.fori_loop(0, NPAT, forward, 0)

    def inverse(m, first, last):
        def one(j, _):
            g0 = left(tab, 0, 0, far[m * NPAT + j, 0] * factor[j, 0])
            g1 = left(tab, 0, 1, far[m * NPAT + j, 1] * factor[j, 1])
            top, bot = g0 + g1, g0 - g1
            xr = jnp.concatenate([top[:HALF], bot[:HALF]], axis=0)
            xi = jnp.concatenate([top[HALF:], bot[HALF:]], axis=0)
            b0 = right(jnp.concatenate([xr[:, :HALF], xi[:, :HALF]], axis=1), tab, 1, 0)
            b1 = right(jnp.concatenate([xr[:, HALF:], xi[:, HALF:]], axis=1), tab, 1, 1)
            lo, hi = b0 + b1, b0 - b1
            br = jnp.concatenate([lo[:, :HALF], hi[:, :HALF]], axis=1)
            bi = jnp.concatenate([lo[:, HALF:], hi[:, HALF:]], axis=1)
            qr, qi = probe[0, m], probe[1, m]
            grad[j, 0] += qr * br + qi * bi
            grad[j, 1] += qr * bi - qi * br
            pr, pi = patch[j, 0], patch[j, 1]
            numer[0, m] += pr * br + pi * bi
            numer[1, m] += pr * bi - pi * br
            return 0

        if first == 0:
            numer[0, m] = jnp.zeros((PAT, PAT), F32)
            numer[1, m] = jnp.zeros((PAT, PAT), F32)
        lax.fori_loop(first, last, one, 0)

    rows = pl.multiple_of(me.plane * 16, 16)
    core_sems, plane_sems, line_sems = (core_send, core_recv), (plane_send, plane_recv), (line_send, line_recv)
    back_line_sems, back_plane_sems = (back_line_send, back_line_recv), (back_plane_send, back_plane_recv)
    back_core_sems, edge_sems = (back_core_send, back_core_recv), (edge_send, edge_recv)

    def core_start(m):
        plane = 0 if m == MODES else 1 - me.core
        send(numer.at[plane, m], from_core.at[m], core_sems, m, me.sibling())

    def plane_start(m):
        await_bytes(from_core.at[m], core_recv.at[m])
        part[m] = numer[0 if m == MODES else me.core, m] + from_core[m]

        def one(k, _):
            device, number = me.in_plane(k)
            there = pl.multiple_of(number * 16, 16)
            send(part.at[m, pl.ds(there, 16), :], from_plane.at[m, k - 1], plane_sems, m, device)
            return 0

        lax.fori_loop(1, 16, one, 0)

    def line_start(m):
        await_bytes(from_plane.at[m], plane_recv.at[m])
        total = part[m, pl.ds(rows, 16), :]
        for k in range(15):
            total = total + from_plane[m, k]
        for k in range(4):
            line[m, k] = total[(k // 2) * 8:(k // 2) * 8 + 8, (k % 2) * HALF:(k % 2 + 1) * HALF]
        for k in range(1, 4):
            device, there = me.on_line(k)
            send(line.at[m, there], from_line.at[m, k - 1], line_sems, m, device)

    def line_end(m):
        await_bytes(from_line.at[m], line_recv.at[m])
        return line[m, me.z] + from_line[m, 0] + from_line[m, 1] + from_line[m, 2]

    def back_start(m):
        total = line_end(m)
        row = pl.multiple_of(me.plane * 16 + (me.z // 2) * 8, 8)
        column = pl.multiple_of(lax.rem(me.z, 2) * HALF, HALF)
        old = probe[me.core, m, pl.ds(row, 8), pl.ds(column, HALF)]
        own[m, me.z] = (old + total) / (own[MODES, 0] + 1.0)
        for k in range(1, 4):
            send(own.at[m, me.z], own.at[m, me.z], back_line_sems, m, me.on_line(k)[0])

    def back_plane_start(m):
        await_bytes(own.at[m, pl.ds(0, 3)], back_line_recv.at[m])
        top = jnp.concatenate([own[m, 0], own[m, 1]], axis=1)
        bot = jnp.concatenate([own[m, 2], own[m, 3]], axis=1)
        fresh[me.core, m, pl.ds(rows, 16), :] = jnp.concatenate([top, bot], axis=0)
        mine = fresh.at[me.core, m, pl.ds(rows, 16), :]

        def one(k, _):
            send(mine, mine, back_plane_sems, m, me.in_plane(k)[0])
            return 0

        lax.fori_loop(1, 16, one, 0)

    def back_core_start(m):
        await_bytes(fresh.at[me.core, m, pl.ds(0, 240), :], back_plane_recv.at[m])
        send(fresh.at[me.core, m], fresh.at[me.core, m], back_core_sems, m, me.sibling())

    def back_end(m):
        await_bytes(fresh.at[1 - me.core, m], back_core_recv.at[m])
        for plane in range(2):
            pltpu.make_async_copy(fresh.at[plane, m], probe_out.at[plane, m], out_sem.at[plane * MODES + m]).start()

    stages = [core_start, plane_start, line_start, back_start, back_plane_start, back_core_start, back_end]

    def spread(j, _):
        rows = pl.ds(pl.multiple_of(j * PAT, PAT), PAT)
        for plane in range(2):
            h, l = split(grad[j, plane])
            h, l = split(dot(h, columns[j]) + dot(l, columns[j]))
            spread_hi[plane, rows, :] = h
            spread_lo[plane, rows, :] = l
        return 0

    def update(start, count):
        for plane in range(2):
            chosen = place_rows[start:start + count, :]
            total = obj[plane, start:start + count, :] + dot(chosen, spread_hi[plane]) + dot(chosen, spread_lo[plane])
            mid[plane, start:start + count, :] = total * inv[start:start + count, :]

    def mask_start():
        send(mask, mask_in, edge_sems, 0, me.region_by(1))

    def edge_start():
        up[...] = mid[:, :EDGE] + dual_top[...]
        low[...] = mid[:, TILE - EDGE:] + dual_bottom[...]
        send(up, from_below, edge_sems, 1, me.region_by(-1))
        send(low, from_above, edge_sems, 2, me.region_by(1))

    def middle_out():
        middle = pl.ds(EDGE, TILE - 2 * EDGE)
        pltpu.make_async_copy(mid.at[:, middle], obj_out.at[:, middle], out_sem.at[8]).start()

    def edge_end():
        await_bytes(mask_in, edge_recv.at[0])
        await_bytes(from_below, edge_recv.at[1])
        await_bytes(from_above, edge_recv.at[2])
        for plane in range(2):
            here = mid[plane, TILE - EDGE:]
            agreed = 0.5 * (low[plane] + from_below[plane])
            active = jnp.broadcast_to(mask[0:1, :], (EDGE, TILE)) > 0.5
            bottom_new[plane] = jnp.where(active, dual_bottom[plane] + (here - agreed), dual_bottom[plane])
            mid[plane, TILE - EDGE:] = jnp.where(active, agreed, here)
            here = mid[plane, :EDGE]
            agreed = 0.5 * (from_above[plane] + up[plane])
            active = jnp.broadcast_to(mask_in[0:1, :], (EDGE, TILE)) > 0.5
            top_new[plane] = jnp.where(active, dual_top[plane] + (here - agreed), dual_top[plane])
            mid[plane, :EDGE] = jnp.where(active, agreed, here)
        for i, part_rows in enumerate((pl.ds(0, EDGE), pl.ds(TILE - EDGE, EDGE))):
            pltpu.make_async_copy(mid.at[:, part_rows], obj_out.at[:, part_rows], out_sem.at[9 + i]).start()
        pltpu.make_async_copy(top_new, top_out, out_sem.at[11]).start()
        pltpu.make_async_copy(bottom_new, bottom_out, out_sem.at[12]).start()

    pl.semaphore_wait(barrier, 21)
    mask_start()
    core_start(MODES)
    for m in range(MODES):
        inverse(m, 0, 2)
        if m == 0:
            plane_start(MODES)
        if m == 1:
            own[MODES, 0] = line_end(MODES)
            plane_start(0)
        if m == 2:
            back_start(0)
            plane_start(1)
        if m == 3:
            back_core_start(0)
            back_start(1)
            plane_start(2)
        inverse(m, 2, 4)
        if m == 0:
            line_start(MODES)
        if m == 1:
            line_start(0)
        if m == 2:
            back_plane_start(0)
            line_start(1)
        if m == 3:
            back_end(0)
            back_plane_start(1)
            line_start(2)
        core_start(m)
    lax.fori_loop(0, NPAT, spread, 0)
    plane_start(3)
    back_core_start(1)
    back_start(2)
    update(0, EDGE)
    update(TILE - EDGE, EDGE)
    edge_start()
    line_start(3)
    back_end(1)
    back_plane_start(2)
    update(EDGE, 192)
    back_start(3)
    update(EDGE + 192, 192)
    middle_out()
    back_core_start(2)
    back_plane_start(3)
    back_end(2)
    edge_end()
    back_core_start(3)
    back_end(3)

    for m in range(SUMS):
        await_bytes(from_core.at[m], core_send.at[m])
        await_bytes(from_plane.at[m], plane_send.at[m])
        await_bytes(from_line.at[m], line_send.at[m])
    for m in range(MODES):
        await_bytes(own.at[m, pl.ds(0, 3)], back_line_send.at[m])
        await_bytes(fresh.at[0, m, pl.ds(0, 240), :], back_plane_send.at[m])
        await_bytes(fresh.at[0, m], back_core_send.at[m])
        for plane in range(2):
            pltpu.make_async_copy(fresh.at[plane, m], probe_out.at[plane, m], out_sem.at[plane * MODES + m]).wait()
    await_bytes(mask, edge_send.at[0])
    await_bytes(up, edge_send.at[1])
    await_bytes(low, edge_send.at[2])
    middle = pl.ds(EDGE, TILE - 2 * EDGE)
    pltpu.make_async_copy(mid.at[:, middle], obj_out.at[:, middle], out_sem.at[8]).wait()
    for i, part_rows in enumerate((pl.ds(0, EDGE), pl.ds(TILE - EDGE, EDGE))):
        pltpu.make_async_copy(mid.at[:, part_rows], obj_out.at[:, part_rows], out_sem.at[9 + i]).wait()
    pltpu.make_async_copy(top_new, top_out, out_sem.at[11]).wait()
    pltpu.make_async_copy(bottom_new, bottom_out, out_sem.at[12]).wait()


def local(object_field, probe, amplitudes, positions, dual_top, dual_bottom, pieces, live):
    tab, perm = tables()
    vmem = pl.BlockSpec(memory_space=pltpu.VMEM)
    smem = pl.BlockSpec(memory_space=pltpu.SMEM)
    hbm = pl.BlockSpec(memory_space=pl.ANY)
    buf = lambda *shape: pltpu.VMEM(shape, F32)
    half = lambda *shape: pltpu.VMEM(shape, BF16)
    dma = lambda *shape: pltpu.SemaphoreType.DMA(shape)
    edge = (2, EDGE, TILE)
    shape = lambda *dims: jax.ShapeDtypeStruct(dims, F32)
    prepared = pl.pallas_call(
        prepare,
        out_shape=(
            shape(NPAT, 2, PAT, PAT), shape(TILE, TILE), jax.ShapeDtypeStruct((NPAT, PAT, TILE), BF16),
            jax.ShapeDtypeStruct((TILE, NPAT * PAT), BF16), shape(8, TILE),
        ),
        in_specs=[smem] * 3 + [vmem] * 2,
        out_specs=(vmem,) * 5,
        scratch_shapes=[buf(3 * PAT, 3 * PAT)],
        compiler_params=pltpu.CompilerParams(vmem_limit_bytes=40 * 1024 * 1024),
    )(positions, pieces, live, object_field, probe)
    return pl.pallas_call(
        kernel,
        out_shape=(shape(2, TILE, TILE), shape(2, MODES, PAT, PAT), shape(*edge), shape(*edge)),
        in_specs=[vmem] * 12,
        out_specs=(hbm,) * 4,
        scratch_shapes=[
            buf(MODES * NPAT, 2, PAT, PAT), buf(NPAT, 2, PAT, PAT), buf(NPAT, 2, PAT, PAT),
            half(2, NPAT * PAT, TILE), half(2, NPAT * PAT, TILE), buf(2, TILE, TILE), buf(2, SUMS, PAT, PAT),
            buf(SUMS, PAT, PAT), buf(SUMS, PAT, PAT), buf(SUMS, 15, 16, PAT), buf(SUMS, 4, 8, HALF), buf(SUMS, 3, 8, HALF),
            buf(SUMS, 4, 8, HALF), buf(2, MODES, PAT, PAT),
            buf(8, TILE), buf(*edge), buf(*edge), buf(*edge), buf(*edge), buf(*edge), buf(*edge),
        ] + [dma(SUMS)] * 12 + [dma(3), dma(3), dma(13)],
        compiler_params=pltpu.CompilerParams(vmem_limit_bytes=60 * 1024 * 1024, collective_id=0, has_side_effects=True),
    )(*prepared, object_field, probe, amplitudes, dual_top, dual_bottom, jnp.asarray(tab), jnp.asarray(perm))


def solution(mesh):
    tiles = P(None, "region", "group")
    return jax.shard_map(
        local,
        mesh=mesh,
        in_specs=(tiles, P(), P("region", "group", None), P("region", "group"), tiles, tiles, P("region", "group"), P("region", "group")),
        out_specs=(tiles, P(), tiles, tiles),
        check_vma=False,
    )
```

```python
import numpy as np
import jax
import jax.numpy as jnp
import ml_dtypes
from jax import lax
from jax.experimental import pallas as pl
from jax.experimental.pallas import tpu as pltpu
from jax.sharding import PartitionSpec as P

F32, BF16 = jnp.float32, jnp.bfloat16
MESH = pl.DeviceIdType.MESH
PAT, TILE, MODES, NPAT, HALF = 256, 512, 4, 4, 128
EDGE, BLOCK, NPIECE, KP = 64, 128, 4, 2
LIMIT = 44
SUMS = MODES + 1


def tables():
    n = np.arange(HALF)[:, None]
    out = []
    for p in range(2):
        k = 2 * np.arange(HALF)[None, :] + p
        angle = 2 * np.pi * ((n * k) % PAT) / PAT
        c, s = np.cos(angle) / 16.0, np.sin(angle) / 16.0
        full = np.block([[c, -s], [s, c]])
        out.append(full)
    full = np.stack([np.stack(out), np.stack([o.T for o in out])]).astype(np.float32)
    hi = full.astype(ml_dtypes.bfloat16)
    lo = (full - hi.astype(np.float32)).astype(ml_dtypes.bfloat16)
    perm = np.zeros((PAT, PAT), np.float32)
    for j in range(PAT):
        perm[2 * (j % HALF) + j // HALF, j] = 1.0
    return np.stack([hi, lo], axis=2), np.stack([perm, perm.T]).astype(ml_dtypes.bfloat16)


def dot(a, b):
    return jnp.dot(a, b, preferred_element_type=F32)


def split(a):
    h = a.astype(BF16)
    return h, (a - h.astype(F32)).astype(BF16)


def right(a, t, d, p):
    h, l = split(a)
    return dot(h, t[d, p, 1]) + dot(h, t[d, p, 0]) + dot(l, t[d, p, 0])


def left(t, d, p, a):
    h, l = split(a)
    return dot(t[d, p, 0], l) + dot(t[d, p, 1], h) + dot(t[d, p, 0], h)


def along(shape, axis):
    return lax.broadcasted_iota(jnp.int32, shape, axis)


def lane_turn(block, by):
    return pltpu.roll(block, by & (HALF - 1), 1)


def row_turn(block, by):
    return pltpu.roll(block, by & 7, 1)


def window(obj, plane, row, col):
    base = pl.multiple_of(jnp.minimum((row >> 3) << 3, TILE - PAT - 8), 8)
    side = pl.multiple_of(jnp.minimum((col >> 7) << 7, TILE - PAT - HALF), HALF)
    down, right_by = row - base, col - side
    block = obj[plane, pl.ds(base, PAT + 8), pl.ds(side, PAT + HALF)]
    block = block.reshape((PAT + 8) // 8, 8, PAT + HALF)
    turned = row_turn(block, 8 - down)
    keep = along((PAT // 8, 8, PAT + HALF), 1) + down < 8
    block = jnp.where(keep, turned[:-1], turned[1:]).reshape(PAT, PAT + HALF)
    parts = [lane_turn(block[:, t * HALF:(t + 1) * HALF], HALF - right_by) for t in range(3)]
    keep = along((PAT, HALF), 1) + right_by < HALF
    return jnp.concatenate([jnp.where(keep, parts[t], parts[t + 1]) for t in range(2)], axis=1)


def prepare(pos, pieces, live, obj_far, patch, shifts, mask, denom, obj, sems):
    copies = []
    for i in range(4):
        rows = (i // 2, pl.ds((i % 2) * PAT, PAT))
        copies.append(pltpu.make_async_copy(obj_far.at[rows], obj.at[rows], sems.at[i]))
        copies[-1].start()
    for j in range(NPAT):
        shifts[j:j + 1, :] = jnp.full((1, TILE), pos[0, j], jnp.int32)
        shifts[NPAT + j:NPAT + j + 1, :] = jnp.full((1, TILE), pos[1, j], jnp.int32)
    first, second, count = pieces[0, 0], pieces[0, 1], live[0, 0]
    has_lower = lax.axis_index("region") < 31
    mask[...] = jnp.zeros_like(mask)
    for b in range(NPIECE):
        active = (((first == b) & (count > 0)) | ((second == b) & (count > 1))) & has_lower
        for i, chosen in enumerate((first == b, second == b, active)):
            value = jnp.where(chosen, 1.0, 0.0).astype(F32)
            mask[i:i + 1, b * BLOCK:(b + 1) * BLOCK] = jnp.full((1, BLOCK), value, F32)
    for copy in copies:
        copy.wait()
    total = jnp.zeros((PAT, PAT), F32)
    for j in range(NPAT):
        pr, pi = window(obj, 0, pos[0, j], pos[1, j]), window(obj, 1, pos[0, j], pos[1, j])
        patch[j, 0] = pr
        patch[j, 1] = pi
        total = total + pr * pr + pi * pi
    denom[...] = total


class Place:
    def __init__(self):
        self.group, self.region = lax.axis_index("group"), lax.axis_index("region")
        core, y_lo = lax.rem(self.group, 2), self.group // 2
        x, z, y_hi = self.region // 8, lax.rem(self.region // 2, 4), lax.rem(self.region, 2)
        y = y_hi * 2 + y_lo
        self.core = core
        self.v, self.u, self.w = x + core * (z - x), y + core * (x - y), z + core * (y - z)
        self.number = self.u * 4 + self.w

    def at(self, v, u, w):
        core = self.core
        x, y, z = v + core * (u - v), u + core * (w - u), w + core * (v - w)
        return (lax.rem(y, 2) * 2 + core, (x * 4 + z) * 2 + y // 2)

    def sibling(self):
        return (self.group + 1 - 2 * self.core, self.region)

    def on_line(self, k):
        v = lax.rem(self.v + k, 4)
        return self.at(v, self.u, self.w), v

    def in_plane(self, k):
        u, w = lax.rem(self.u + k // 4, 4), lax.rem(self.w + lax.rem(k, 4), 4)
        return self.at(self.v, u, w), u * 4 + w

    def region_by(self, by):
        return (self.group, lax.rem(self.region + 32 + by, 32))


def send(src, dst, sems, index, device):
    copy = pltpu.make_async_remote_copy(
        src_ref=src, dst_ref=dst, send_sem=sems[0].at[index], recv_sem=sems[1].at[index], device_id=device, device_id_type=MESH
    )
    copy.start()


def await_bytes(ref, sem):
    pltpu.make_async_copy(ref, ref, sem).wait()


def packed(block, hot):
    out = []
    for slot in range(KP):
        chosen = block[:, :BLOCK]
        for b in range(1, NPIECE):
            flag = jnp.broadcast_to(hot[slot:slot + 1, b * BLOCK:(b + 1) * BLOCK], chosen.shape)
            chosen = jnp.where(flag > 0.5, block[:, b * BLOCK:(b + 1) * BLOCK], chosen)
        out.append(chosen)
    return jnp.concatenate(out, axis=1)


def unpacked(block, hot):
    flag = jnp.broadcast_to(hot[0:1, :], (block.shape[0], TILE)) > 0.5
    first = jnp.concatenate([block[:, :BLOCK]] * NPIECE, axis=1)
    second = jnp.concatenate([block[:, BLOCK:]] * NPIECE, axis=1)
    return jnp.where(flag, first, second)


def kernel(
    patch, shifts, mask, denom, probe, tab, far_obj, far_amp, far_perm, far_top, far_bottom,
    mid, probe_out, top_out, bottom_out,
    far, factor, grad, spread_hi, spread_lo, numer,
    from_core, part, from_line, block, from_plane, tiles, fresh, scale,
    obj, amp, perm, dual_top, dual_bottom, mask_in, up, low, up_sent, low_sent, from_below, from_above,
    core_send, core_recv, line_send, line_recv, plane_send, plane_recv,
    back_plane_send, back_plane_recv, back_line_send, back_line_recv, back_core_send, back_core_recv,
    edge_send, edge_recv, load_sem,
):
    loads = [
        pltpu.make_async_copy(source, target, load_sem.at[i])
        for i, (source, target) in enumerate(
            ((far_perm, perm), (far_amp, amp), (far_obj, obj), (far_top, dual_top), (far_bottom, dual_bottom))
        )
    ]
    for load in loads:
        load.start()
    me = Place()
    barrier = pltpu.get_barrier_semaphore()

    def greet(device):
        pl.semaphore_signal(barrier, inc=1, device_id=device, device_id_type=MESH)

    greet(me.sibling())
    for k in range(1, 4):
        greet(me.on_line(k)[0])
    for k in range(1, 16):
        greet(me.in_plane(k)[0])
    greet(me.region_by(1))
    greet(me.region_by(-1))

    grad[...] = jnp.zeros_like(grad)

    def forward(j, _):
        pr, pi = patch[j, 0], patch[j, 1]

        def mode(m, _):
            pr, pi = patch[j, 0], patch[j, 1]
            qr, qi = probe[0, m], probe[1, m]
            er = qr * pr - qi * pi
            ei = qr * pi + qi * pr
            lo = jnp.concatenate([er[:, :HALF], ei[:, :HALF]], axis=1)
            hi = jnp.concatenate([er[:, HALF:], ei[:, HALF:]], axis=1)
            y0 = right(lo + hi, tab, 0, 0)
            y1 = right(lo - hi, tab, 0, 1)
            yr = jnp.concatenate([y0[:, :HALF], y1[:, :HALF]], axis=1)
            yi = jnp.concatenate([y0[:, HALF:], y1[:, HALF:]], axis=1)
            top = jnp.concatenate([yr[:HALF], yi[:HALF]], axis=0)
            bot = jnp.concatenate([yr[HALF:], yi[HALF:]], axis=0)
            far[m * NPAT + j, 0] = left(tab, 1, 0, top + bot)
            far[m * NPAT + j, 1] = left(tab, 1, 1, top - bot)
            return 0

        lax.fori_loop(0, MODES, mode, 0, unroll=True)
        h, l = split(amp[j])
        h, l = split(dot(h, perm[0]) + dot(l, perm[0]))
        full = dot(perm[1], h) + dot(perm[1], l)
        for q in range(2):
            power = jnp.zeros((HALF, PAT), F32)
            for m in range(MODES):
                z = far[m * NPAT + j, q]
                power = power + z[:HALF] * z[:HALF] + z[HALF:] * z[HALF:]
            f = full[q * HALF:(q + 1) * HALF] / jnp.maximum(jnp.sqrt(power), 0.5)
            factor[j, q, :HALF] = f
            factor[j, q, HALF:] = f
        return 0

    def inverse(m, first, last):
        def one(j, _):
            g0 = left(tab, 0, 0, far[m * NPAT + j, 0] * factor[j, 0])
            g1 = left(tab, 0, 1, far[m * NPAT + j, 1] * factor[j, 1])
            top, bot = g0 + g1, g0 - g1
            xr = jnp.concatenate([top[:HALF], bot[:HALF]], axis=0)
            xi = jnp.concatenate([top[HALF:], bot[HALF:]], axis=0)
            b0 = right(jnp.concatenate([xr[:, :HALF], xi[:, :HALF]], axis=1), tab, 1, 0)
            b1 = right(jnp.concatenate([xr[:, HALF:], xi[:, HALF:]], axis=1), tab, 1, 1)
            lo, hi = b0 + b1, b0 - b1
            br = jnp.concatenate([lo[:, :HALF], hi[:, :HALF]], axis=1)
            bi = jnp.concatenate([lo[:, HALF:], hi[:, HALF:]], axis=1)
            qr, qi = probe[0, m], probe[1, m]
            grad[j, 0] += qr * br + qi * bi
            grad[j, 1] += qr * bi - qi * br
            pr, pi = patch[j, 0], patch[j, 1]
            numer[0, m] += pr * br + pi * bi
            numer[1, m] += pr * bi - pi * br
            return 0

        if first == 0:
            numer[0, m] = jnp.zeros((PAT, PAT), F32)
            numer[1, m] = jnp.zeros((PAT, PAT), F32)
        lax.fori_loop(first, last, one, 0, unroll=True)

    line_rows = pl.ds(pl.multiple_of(me.v * 64, 64), 64)
    core_sems, line_sems, plane_sems = (core_send, core_recv), (line_send, line_recv), (plane_send, plane_recv)
    back_plane_sems, back_line_sems = (back_plane_send, back_plane_recv), (back_line_send, back_line_recv)
    back_core_sems, edge_sems = (back_core_send, back_core_recv), (edge_send, edge_recv)

    def mine(m):
        return denom[...] if m == MODES else numer[me.core, m]

    def core_start(m):
        send(denom if m == MODES else numer.at[1 - me.core, m], from_core.at[m], core_sems, m, me.sibling())

    def line_start(m):
        await_bytes(from_core.at[m], core_recv.at[m])
        part[m] = mine(m) + from_core[m]
        for k in range(1, 4):
            device, there = me.on_line(k)
            source = part.at[m, pl.ds(pl.multiple_of(there * 64, 64), 64), :]
            send(source, from_line.at[m, k - 1], line_sems, m, device)

    def plane_start(m):
        await_bytes(from_line.at[m], line_recv.at[m])
        total = part[m, line_rows, :] + from_line[m, 0] + from_line[m, 1] + from_line[m, 2]
        for k in range(16):
            block[m, k] = total[(k // 2) * 8:(k // 2) * 8 + 8, (k % 2) * HALF:(k % 2 + 1) * HALF]

        for k in range(1, 16):
            device, there = me.in_plane(k)
            send(block.at[m, there], from_plane.at[m, k - 1], plane_sems, m, device)

    def total_of(m):
        await_bytes(from_plane.at[m], plane_recv.at[m])
        total = block[m, me.number]
        for k in range(15):
            total = total + from_plane[m, k]
        return total

    def denom_end():
        scale[...] = total_of(MODES) + 1.0

    def back_start(m):
        row = pl.multiple_of(me.v * 64 + (me.number // 2) * 8, 8)
        column = pl.multiple_of(lax.rem(me.number, 2) * HALF, HALF)
        old = probe[me.core, m, pl.ds(row, 8), pl.ds(column, HALF)]
        tiles[m, me.number] = (old + total_of(m)) / scale[...]
        own = tiles.at[m, me.number]

        for k in range(1, 16):
            send(own, own, back_plane_sems, m, me.in_plane(k)[0])

    def back_line_start(m):
        await_bytes(tiles.at[m, pl.ds(0, 15)], back_plane_recv.at[m])
        rows = [jnp.concatenate([tiles[m, 2 * i], tiles[m, 2 * i + 1]], axis=1) for i in range(8)]
        fresh[me.core, m, line_rows, :] = jnp.concatenate(rows, axis=0)
        own = fresh.at[me.core, m, line_rows, :]
        for k in range(1, 4):
            send(own, own, back_line_sems, m, me.on_line(k)[0])

    def back_core_start(m):
        await_bytes(fresh.at[me.core, m, pl.ds(0, 192), :], back_line_recv.at[m])
        send(fresh.at[me.core, m], fresh.at[me.core, m], back_core_sems, m, me.sibling())

    def back_end(m):
        await_bytes(fresh.at[1 - me.core, m], back_core_recv.at[m])
        for plane in range(2):
            probe_out[plane, m] = fresh[plane, m]

    def spread_plane(plane, j, block):
        rows = pl.ds(pl.multiple_of(j * PAT, PAT), PAT)
        by = jnp.broadcast_to(shifts[pl.ds(NPAT + j, 1), :], (PAT, TILE))
        columns = jnp.where(along((PAT, TILE), 1) - along((PAT, TILE), 0) == by, 1.0, 0.0).astype(BF16)
        h, l = split(block)
        h, l = split(dot(h, columns) + dot(l, columns))
        spread_hi[plane, rows, :] = h
        spread_lo[plane, rows, :] = l

    def spread(first, last):
        def one(j, _):
            spread_plane(0, j, grad[j, 0])
            spread_plane(1, j, grad[j, 1])
            return 0

        lax.fori_loop(first, last, one, 0, unroll=True)

    def spread_weights():
        power = sum(probe[0, m] * probe[0, m] + probe[1, m] * probe[1, m] for m in range(MODES))
        for j in range(NPAT):
            spread_plane(2, j, power)

    def update(starts, count):
        chosen = []
        for j in range(NPAT):
            by = jnp.broadcast_to(shifts[j:j + 1, :PAT], (count, PAT))
            away = along((count, PAT), 0) - along((count, PAT), 1)
            chosen.append(jnp.concatenate([jnp.where(away + start == by, 1.0, 0.0).astype(BF16) for start in starts], axis=0))
        chosen = jnp.concatenate(chosen, axis=1)
        sums = [dot(chosen, spread_hi[plane]) + dot(chosen, spread_lo[plane]) for plane in range(3)]
        for i, start in enumerate(starts):
            rows, here = slice(start, start + count), slice(i * count, (i + 1) * count)
            inverse_weight = 1.0 / (sums[2][here] + 1.0)
            for plane in range(2):
                mid[plane, rows, :] = (obj[plane, rows, :] + sums[plane][here]) * inverse_weight

    def mask_start():
        send(mask, mask_in, edge_sems, 0, me.region_by(1))

    def edge_start():
        await_bytes(mask_in, edge_recv.at[0])
        for plane in range(2):
            up[plane] = mid[plane, :EDGE] + dual_top[plane]
            low[plane] = mid[plane, TILE - EDGE:] + dual_bottom[plane]
            up_sent[plane] = packed(up[plane], mask_in)
            low_sent[plane] = packed(low[plane], mask)
        send(up_sent, from_below, edge_sems, 1, me.region_by(-1))
        send(low_sent, from_above, edge_sems, 2, me.region_by(1))

    def edge_end():
        await_bytes(from_below, edge_recv.at[1])
        await_bytes(from_above, edge_recv.at[2])
        for plane in range(2):
            here = mid[plane, TILE - EDGE:]
            agreed = 0.5 * (low[plane] + unpacked(from_below[plane], mask))
            active = jnp.broadcast_to(mask[2:3, :], (EDGE, TILE)) > 0.5
            bottom_out[plane] = jnp.where(active, dual_bottom[plane] + (here - agreed), dual_bottom[plane])
            mid[plane, TILE - EDGE:] = jnp.where(active, agreed, here)
            here = mid[plane, :EDGE]
            agreed = 0.5 * (unpacked(from_above[plane], mask_in) + up[plane])
            active = jnp.broadcast_to(mask_in[2:3, :], (EDGE, TILE)) > 0.5
            top_out[plane] = jnp.where(active, dual_top[plane] + (here - agreed), dual_top[plane])
            mid[plane, :EDGE] = jnp.where(active, agreed, here)

    loads[0].wait()
    loads[1].wait()
    lax.fori_loop(0, 1, forward, 0)
    lax.fori_loop(1, 2, forward, 0)
    lax.fori_loop(2, 3, forward, 0)
    pl.semaphore_wait(barrier, 21)
    mask_start()
    core_start(MODES)
    lax.fori_loop(3, 4, forward, 0)
    line_start(MODES)
    inverse(0, 0, 4)
    core_start(0)
    inverse(1, 0, 2)
    line_start(0)
    plane_start(MODES)
    inverse(1, 2, 4)
    core_start(1)
    inverse(2, 0, 2)
    line_start(1)
    inverse(2, 2, 4)
    core_start(2)
    plane_start(0)
    inverse(3, 0, 2)
    line_start(2)
    inverse(3, 2, 4)
    core_start(3)
    denom_end()
    spread(0, 2)
    plane_start(1)
    spread(2, 4)
    line_start(3)
    back_start(0)
    spread_weights()
    plane_start(2)
    for load in loads[2:]:
        load.wait()
    update((0, TILE - EDGE), EDGE)
    edge_start()
    back_start(1)
    update((EDGE,), TILE // 2 - EDGE)
    plane_start(3)
    update((TILE // 2,), TILE // 2 - EDGE)
    back_line_start(0)
    back_start(2)
    back_line_start(1)
    back_start(3)
    back_core_start(0)
    back_line_start(2)
    edge_end()
    back_end(0)
    back_core_start(1)
    back_line_start(3)
    back_end(1)
    back_core_start(2)
    back_end(2)
    back_core_start(3)
    back_end(3)

    for m in range(SUMS):
        await_bytes(from_core.at[m], core_send.at[m])
        await_bytes(from_line.at[m], line_send.at[m])
        await_bytes(from_plane.at[m], plane_send.at[m])
    for m in range(MODES):
        await_bytes(tiles.at[m, pl.ds(0, 15)], back_plane_send.at[m])
        await_bytes(fresh.at[0, m, pl.ds(0, 192), :], back_line_send.at[m])
        await_bytes(fresh.at[0, m], back_core_send.at[m])
    await_bytes(mask_in, edge_send.at[0])
    await_bytes(up_sent, edge_send.at[1])
    await_bytes(low_sent, edge_send.at[2])


def local(object_field, probe, amplitudes, positions, dual_top, dual_bottom, pieces, live):
    tab, perm = tables()
    vmem = pl.BlockSpec(memory_space=pltpu.VMEM)
    smem = pl.BlockSpec(memory_space=pltpu.SMEM)
    far = pl.BlockSpec(memory_space=pl.ANY)
    buf = lambda *shape: pltpu.VMEM(shape, F32)
    half = lambda *shape: pltpu.VMEM(shape, BF16)
    dma = lambda *shape: pltpu.SemaphoreType.DMA(shape)
    edge, sent = (2, EDGE, TILE), (2, EDGE, KP * BLOCK)
    shape = lambda *dims: jax.ShapeDtypeStruct(dims, F32)
    prepared = pl.pallas_call(
        prepare,
        out_shape=(shape(NPAT, 2, PAT, PAT), jax.ShapeDtypeStruct((2 * NPAT, TILE), jnp.int32), shape(8, TILE), shape(PAT, PAT)),
        in_specs=[smem] * 3 + [far],
        out_specs=(vmem,) * 4,
        scratch_shapes=[buf(2, TILE, TILE), dma(4)],
        compiler_params=pltpu.CompilerParams(vmem_limit_bytes=16 * 1024 * 1024),
    )(positions.T, pieces.T, live, object_field)
    return pl.pallas_call(
        kernel,
        out_shape=(shape(2, TILE, TILE), shape(2, MODES, PAT, PAT), shape(*edge), shape(*edge)),
        in_specs=[vmem] * 6 + [far] * 5,
        out_specs=(vmem,) * 4,
        scratch_shapes=[
            buf(MODES * NPAT, 2, PAT, PAT), buf(NPAT, 2, PAT, PAT), buf(NPAT, 2, PAT, PAT),
            half(3, NPAT * PAT, TILE), half(3, NPAT * PAT, TILE), buf(2, MODES, PAT, PAT),
            buf(SUMS, PAT, PAT), buf(SUMS, PAT, PAT), buf(SUMS, 3, 64, PAT), buf(SUMS, 16, 8, HALF), buf(SUMS, 15, 8, HALF),
            buf(MODES, 16, 8, HALF), buf(2, MODES, PAT, PAT), buf(8, HALF),
            buf(2, TILE, TILE), buf(NPAT, PAT, PAT), half(2, PAT, PAT), buf(*edge), buf(*edge),
            buf(8, TILE), buf(*edge), buf(*edge), buf(*sent), buf(*sent), buf(*sent), buf(*sent),
        ] + [dma(SUMS)] * 6 + [dma(MODES)] * 6 + [dma(3), dma(3), dma(5)],
        compiler_params=pltpu.CompilerParams(vmem_limit_bytes=LIMIT * 1024 * 1024, collective_id=0, has_side_effects=True),
    )(*prepared, probe, jnp.asarray(tab), object_field, amplitudes, jnp.asarray(perm), dual_top, dual_bottom)


def solution(mesh):
    tiles = P(None, "region", "group")
    return jax.shard_map(
        local,
        mesh=mesh,
        in_specs=(tiles, P(), P("region", "group", None), P("region", "group"), tiles, tiles, P("region", "group"), P("region", "group")),
        out_specs=(tiles, P(), tiles, tiles),
        check_vma=False,
    )
```

```python
import numpy as np
import jax
import jax.numpy as jnp
import ml_dtypes
from jax import lax
from jax.experimental import pallas as pl
from jax.experimental.pallas import tpu as pltpu
from jax.sharding import PartitionSpec as P

F32, BF16 = jnp.float32, jnp.bfloat16
MESH = pl.DeviceIdType.MESH
PAT, TILE, MODES, NPAT, HALF = 256, 512, 4, 4, 128
EDGE, BLOCK, NPIECE, KP = 64, 128, 4, 2
LOADS = 21
LIMIT = 46
POWER, DUALS = NPAT * PAT, (NPAT + 1) * PAT
SUMS = MODES + 1


def tables():
    n = np.arange(HALF)[:, None]
    out = []
    for p in range(2):
        k = 2 * np.arange(HALF)[None, :] + p
        angle = 2 * np.pi * ((n * k) % PAT) / PAT
        c, s = np.cos(angle) / 16.0, np.sin(angle) / 16.0
        full = np.block([[c, -s], [s, c]])
        out.append(full)
    full = np.stack([np.stack(out), np.stack([o.T for o in out])]).astype(np.float32)
    hi = full.astype(ml_dtypes.bfloat16)
    lo = (full - hi.astype(np.float32)).astype(ml_dtypes.bfloat16)
    return np.stack([hi, lo], axis=2)


def dot(a, b):
    return jnp.dot(a, b, preferred_element_type=F32)


def split(a):
    h = a.astype(BF16)
    return h, (a - h.astype(F32)).astype(BF16)


def right(a, t, d, p):
    h, l = split(a)
    return dot(h, t[d, p, 1]) + dot(h, t[d, p, 0]) + dot(l, t[d, p, 0])


def left(t, d, p, a):
    h, l = split(a)
    return dot(t[d, p, 0], l) + dot(t[d, p, 1], h) + dot(t[d, p, 0], h)


def along(shape, axis):
    return lax.broadcasted_iota(jnp.int32, shape, axis)


def lane_turn(block, by):
    return pltpu.roll(block, by & (HALF - 1), 1)


def row_turn(block, by):
    return pltpu.roll(block, by & 7, 1)


def window(obj, plane, row, col):
    base = pl.multiple_of(jnp.minimum((row >> 3) << 3, TILE - PAT - 8), 8)
    side = pl.multiple_of(jnp.minimum((col >> 7) << 7, TILE - PAT - HALF), HALF)
    down, right_by = row - base, col - side
    block = obj[plane, pl.ds(base, PAT + 8), pl.ds(side, PAT + HALF)]
    block = block.reshape((PAT + 8) // 8, 8, PAT + HALF)
    turned = row_turn(block, 8 - down)
    keep = along((PAT // 8, 8, PAT + HALF), 1) + down < 8
    block = jnp.where(keep, turned[:-1], turned[1:]).reshape(PAT, PAT + HALF)
    parts = [lane_turn(block[:, t * HALF:(t + 1) * HALF], HALF - right_by) for t in range(3)]
    keep = along((PAT, HALF), 1) + right_by < HALF
    return jnp.concatenate([jnp.where(keep, parts[t], parts[t + 1]) for t in range(2)], axis=1)


def prepare(pos, far_obj, far_top, far_bottom, work_out, work, obj, sems):
    loads, stores = [], []
    for i in range(4):
        rows = (i // 2, pl.ds((i % 2) * PAT, PAT))
        loads.append(pltpu.make_async_copy(far_obj.at[rows], obj.at[rows], sems.at[i]))
    for i, source in enumerate((far_top.at[0], far_top.at[1], far_bottom.at[0], far_bottom.at[1])):
        loads.append(pltpu.make_async_copy(source, work.at[pl.ds(DUALS + i * EDGE, EDGE)], sems.at[4 + i]))
    for copy in loads:
        copy.start()
    for j in range(NPAT):
        work[POWER + j:POWER + j + 1, PAT:] = jnp.full((1, PAT), pos[0, j].astype(F32), F32)
        work[POWER + NPAT + j:POWER + NPAT + j + 1, PAT:] = jnp.full((1, PAT), pos[1, j].astype(F32), F32)
    for copy in loads[:4]:
        copy.wait()
    total = jnp.zeros((PAT, PAT), F32)
    for j in range(NPAT):
        pr, pi = window(obj, 0, pos[0, j], pos[1, j]), window(obj, 1, pos[0, j], pos[1, j])
        rows = pl.ds(j * PAT, PAT)
        work[rows, :PAT] = pr
        work[rows, PAT:] = pi
        stores.append(pltpu.make_async_copy(work.at[rows], work_out.at[rows], sems.at[8 + j]))
        stores[-1].start()
        total = total + pr * pr + pi * pi
    work[POWER:POWER + PAT, :PAT] = total
    for copy in loads[4:]:
        copy.wait()
    rows = pl.ds(POWER, 2 * PAT)
    stores.append(pltpu.make_async_copy(work.at[rows], work_out.at[rows], sems.at[12]))
    stores[-1].start()
    for copy in stores:
        copy.wait()


class Place:
    def __init__(self):
        self.group, self.region = lax.axis_index("group"), lax.axis_index("region")
        core, y_lo = lax.rem(self.group, 2), self.group // 2
        x, z, y_hi = self.region // 8, lax.rem(self.region // 2, 4), lax.rem(self.region, 2)
        y = y_hi * 2 + y_lo
        self.core = core
        self.v, self.u, self.w = x + core * (z - x), y + core * (x - y), z + core * (y - z)
        self.number = self.u * 4 + self.w

    def at(self, v, u, w):
        core = self.core
        x, y, z = v + core * (u - v), u + core * (w - u), w + core * (v - w)
        return (lax.rem(y, 2) * 2 + core, (x * 4 + z) * 2 + y // 2)

    def sibling(self):
        return (self.group + 1 - 2 * self.core, self.region)

    def on_line(self, k):
        v = lax.rem(self.v + k, 4)
        return self.at(v, self.u, self.w), v

    def in_plane(self, k):
        u, w = lax.rem(self.u + k // 4, 4), lax.rem(self.w + lax.rem(k, 4), 4)
        return self.at(self.v, u, w), u * 4 + w

    def region_by(self, by):
        return (self.group, lax.rem(self.region + 32 + by, 32))


def send(src, dst, sems, index, device):
    copy = pltpu.make_async_remote_copy(
        src_ref=src, dst_ref=dst, send_sem=sems[0].at[index], recv_sem=sems[1].at[index], device_id=device, device_id_type=MESH
    )
    copy.start()


def await_bytes(ref, sem):
    pltpu.make_async_copy(ref, ref, sem).wait()


def packed(block, hot):
    out = []
    for slot in range(KP):
        chosen = block[:, :BLOCK]
        for b in range(1, NPIECE):
            flag = jnp.broadcast_to(hot[slot:slot + 1, b * BLOCK:(b + 1) * BLOCK], chosen.shape)
            chosen = jnp.where(flag > 0.5, block[:, b * BLOCK:(b + 1) * BLOCK], chosen)
        out.append(chosen)
    return jnp.concatenate(out, axis=1)


def unpacked(block, hot):
    flag = jnp.broadcast_to(hot[0:1, :], (block.shape[0], TILE)) > 0.5
    first = jnp.concatenate([block[:, :BLOCK]] * NPIECE, axis=1)
    second = jnp.concatenate([block[:, BLOCK:]] * NPIECE, axis=1)
    return jnp.where(flag, first, second)


def kernel(
    far_work, far_probe, far_tab, pieces, live, far_obj, far_amp,
    mid, probe_out, top_out, bottom_out,
    far, factor, grad, spread_hi, spread_lo, numer,
    from_core, part, from_line, block, from_plane, tiles, fresh, scale,
    work, denom, probe, tab, obj, amp, perm, mask, mask_in, up, low, up_sent, low_sent, from_below, from_above,
    core_send, core_recv, line_send, line_recv, plane_send, plane_recv,
    back_plane_send, back_plane_recv, back_line_send, back_line_recv, back_core_send, back_core_recv,
    edge_send, edge_recv, load_sem,
):
    pairs = [(far_work.at[pl.ds(j * PAT, PAT)], work.at[pl.ds(j * PAT, PAT)]) for j in range(NPAT + 2)]
    pairs = [(far_tab, tab)] + [(far_probe.at[plane, m], probe.at[plane, m]) for m in range(MODES) for plane in range(2)] + pairs
    pairs += [(far_amp.at[j], amp.at[j]) for j in range(NPAT)] + [(far_obj.at[plane], obj.at[plane]) for plane in range(2)]
    loads = [pltpu.make_async_copy(source, target, load_sem.at[i]) for i, (source, target) in enumerate(pairs)]
    for load in loads:
        load.start()

    def wait_loads(first, last):
        for load in loads[first:last]:
            load.wait()

    me = Place()
    barrier = pltpu.get_barrier_semaphore()

    def greet(device):
        pl.semaphore_signal(barrier, inc=1, device_id=device, device_id_type=MESH)

    greet(me.sibling())
    for k in range(1, 4):
        greet(me.on_line(k)[0])
    for k in range(1, 16):
        greet(me.in_plane(k)[0])
    greet(me.region_by(1))
    greet(me.region_by(-1))

    for i, (axis, other) in enumerate(((1, 0), (0, 1))):
        place = along((PAT, PAT), axis)
        source = 2 * (place & (HALF - 1)) + (place >> 7)
        perm[i] = jnp.where(along((PAT, PAT), other) == source, 1.0, 0.0).astype(BF16)
    grad[...] = jnp.zeros_like(grad)

    def window_of(j):
        rows = pl.ds(pl.multiple_of(j * PAT, PAT), PAT)
        return work[rows, :PAT], work[rows, PAT:]

    def forward(j, _):
        pr, pi = window_of(j)

        def mode(m, _):
            pr, pi = window_of(j)
            qr, qi = probe[0, m], probe[1, m]
            er = qr * pr - qi * pi
            ei = qr * pi + qi * pr
            lo = jnp.concatenate([er[:, :HALF], ei[:, :HALF]], axis=1)
            hi = jnp.concatenate([er[:, HALF:], ei[:, HALF:]], axis=1)
            y0 = right(lo + hi, tab, 0, 0)
            y1 = right(lo - hi, tab, 0, 1)
            yr = jnp.concatenate([y0[:, :HALF], y1[:, :HALF]], axis=1)
            yi = jnp.concatenate([y0[:, HALF:], y1[:, HALF:]], axis=1)
            top = jnp.concatenate([yr[:HALF], yi[:HALF]], axis=0)
            bot = jnp.concatenate([yr[HALF:], yi[HALF:]], axis=0)
            far[m * NPAT + j, 0] = left(tab, 1, 0, top + bot)
            far[m * NPAT + j, 1] = left(tab, 1, 1, top - bot)
            return 0

        lax.fori_loop(0, MODES, mode, 0, unroll=True)
        h, l = split(amp[j])
        h, l = split(dot(h, perm[0]) + dot(l, perm[0]))
        full = dot(perm[1], h) + dot(perm[1], l)
        for q in range(2):
            power = jnp.zeros((HALF, PAT), F32)
            for m in range(MODES):
                z = far[m * NPAT + j, q]
                power = power + z[:HALF] * z[:HALF] + z[HALF:] * z[HALF:]
            f = full[q * HALF:(q + 1) * HALF] / jnp.maximum(jnp.sqrt(power), 0.5)
            factor[j, q, :HALF] = f
            factor[j, q, HALF:] = f
        return 0

    def inverse(m, first, last):
        def one(j, _):
            g0 = left(tab, 0, 0, far[m * NPAT + j, 0] * factor[j, 0])
            g1 = left(tab, 0, 1, far[m * NPAT + j, 1] * factor[j, 1])
            top, bot = g0 + g1, g0 - g1
            xr = jnp.concatenate([top[:HALF], bot[:HALF]], axis=0)
            xi = jnp.concatenate([top[HALF:], bot[HALF:]], axis=0)
            b0 = right(jnp.concatenate([xr[:, :HALF], xi[:, :HALF]], axis=1), tab, 1, 0)
            b1 = right(jnp.concatenate([xr[:, HALF:], xi[:, HALF:]], axis=1), tab, 1, 1)
            lo, hi = b0 + b1, b0 - b1
            br = jnp.concatenate([lo[:, :HALF], hi[:, :HALF]], axis=1)
            bi = jnp.concatenate([lo[:, HALF:], hi[:, HALF:]], axis=1)
            qr, qi = probe[0, m], probe[1, m]
            grad[j, 0] += qr * br + qi * bi
            grad[j, 1] += qr * bi - qi * br
            pr, pi = window_of(j)
            numer[0, m] += pr * br + pi * bi
            numer[1, m] += pr * bi - pi * br
            return 0

        if first == 0:
            numer[0, m] = jnp.zeros((PAT, PAT), F32)
            numer[1, m] = jnp.zeros((PAT, PAT), F32)
        lax.fori_loop(first, last, one, 0, unroll=True)

    line_rows = pl.ds(pl.multiple_of(me.v * 64, 64), 64)
    core_sems, line_sems, plane_sems = (core_send, core_recv), (line_send, line_recv), (plane_send, plane_recv)
    back_plane_sems, back_line_sems = (back_plane_send, back_plane_recv), (back_line_send, back_line_recv)
    back_core_sems, edge_sems = (back_core_send, back_core_recv), (edge_send, edge_recv)

    def mine(m):
        return denom[...] if m == MODES else numer[me.core, m]

    def core_start(m):
        send(denom if m == MODES else numer.at[1 - me.core, m], from_core.at[m], core_sems, m, me.sibling())

    def line_start(m):
        await_bytes(from_core.at[m], core_recv.at[m])
        part[m] = mine(m) + from_core[m]
        for k in range(1, 4):
            device, there = me.on_line(k)
            source = part.at[m, pl.ds(pl.multiple_of(there * 64, 64), 64), :]
            send(source, from_line.at[m, k - 1], line_sems, m, device)

    def plane_start(m):
        await_bytes(from_line.at[m], line_recv.at[m])
        total = part[m, line_rows, :] + from_line[m, 0] + from_line[m, 1] + from_line[m, 2]
        for k in range(16):
            block[m, k] = total[(k // 2) * 8:(k // 2) * 8 + 8, (k % 2) * HALF:(k % 2 + 1) * HALF]

        for k in range(1, 16):
            device, there = me.in_plane(k)
            send(block.at[m, there], from_plane.at[m, k - 1], plane_sems, m, device)

    def total_of(m):
        await_bytes(from_plane.at[m], plane_recv.at[m])
        total = block[m, me.number]
        for k in range(15):
            total = total + from_plane[m, k]
        return total

    def denom_end():
        scale[...] = total_of(MODES) + 1.0

    def back_start(m):
        row = pl.multiple_of(me.v * 64 + (me.number // 2) * 8, 8)
        column = pl.multiple_of(lax.rem(me.number, 2) * HALF, HALF)
        old = probe[me.core, m, pl.ds(row, 8), pl.ds(column, HALF)]
        tiles[m, me.number] = (old + total_of(m)) / scale[...]
        own = tiles.at[m, me.number]

        for k in range(1, 16):
            send(own, own, back_plane_sems, m, me.in_plane(k)[0])

    def back_line_start(m):
        await_bytes(tiles.at[m, pl.ds(0, 15)], back_plane_recv.at[m])
        rows = [jnp.concatenate([tiles[m, 2 * i], tiles[m, 2 * i + 1]], axis=1) for i in range(8)]
        fresh[me.core, m, line_rows, :] = jnp.concatenate(rows, axis=0)
        own = fresh.at[me.core, m, line_rows, :]
        for k in range(1, 4):
            send(own, own, back_line_sems, m, me.on_line(k)[0])

    def back_core_start(m):
        await_bytes(fresh.at[me.core, m, pl.ds(0, 192), :], back_line_recv.at[m])
        send(fresh.at[me.core, m], fresh.at[me.core, m], back_core_sems, m, me.sibling())

    def back_end(m):
        await_bytes(fresh.at[1 - me.core, m], back_core_recv.at[m])
        for plane in range(2):
            probe_out[plane, m] = fresh[plane, m]

    def spread_plane(plane, j, block):
        rows = pl.ds(pl.multiple_of(j * PAT, PAT), PAT)
        by = jnp.broadcast_to(work[pl.ds(POWER + NPAT + j, 1), PAT:], (PAT, PAT)).astype(jnp.int32)
        by = jnp.concatenate([by, by], axis=1)
        columns = jnp.where(along((PAT, TILE), 1) - along((PAT, TILE), 0) == by, 1.0, 0.0).astype(BF16)
        h, l = split(block)
        h, l = split(dot(h, columns) + dot(l, columns))
        spread_hi[plane, rows, :] = h
        spread_lo[plane, rows, :] = l

    def spread(first, last):
        def one(j, _):
            spread_plane(0, j, grad[j, 0])
            spread_plane(1, j, grad[j, 1])
            return 0

        lax.fori_loop(first, last, one, 0, unroll=True)

    def spread_weights():
        power = sum(probe[0, m] * probe[0, m] + probe[1, m] * probe[1, m] for m in range(MODES))
        for j in range(NPAT):
            spread_plane(2, j, power)

    def update(starts, count):
        chosen = []
        for j in range(NPAT):
            by = jnp.broadcast_to(work[POWER + j:POWER + j + 1, PAT:], (count, PAT)).astype(jnp.int32)
            away = along((count, PAT), 0) - along((count, PAT), 1)
            chosen.append(jnp.concatenate([jnp.where(away + start == by, 1.0, 0.0).astype(BF16) for start in starts], axis=0))
        chosen = jnp.concatenate(chosen, axis=1)
        sums = [dot(chosen, spread_hi[plane]) + dot(chosen, spread_lo[plane]) for plane in range(3)]
        for i, start in enumerate(starts):
            rows, here = slice(start, start + count), slice(i * count, (i + 1) * count)
            inverse_weight = 1.0 / (sums[2][here] + 1.0)
            for plane in range(2):
                mid[plane, rows, :] = (obj[plane, rows, :] + sums[plane][here]) * inverse_weight

    def dual(side, plane):
        start = DUALS + (2 * side + plane) * EDGE
        return work[start:start + EDGE, :]

    def mask_start():
        wide = lambda ref, i: jnp.broadcast_to(ref[0:1, i:i + 1], (1, TILE))
        number = along((1, TILE), 1) // BLOCK
        first, second, count = wide(pieces, 0) == number, wide(pieces, 1) == number, wide(live, 0)
        last = jnp.broadcast_to(me.region, (1, TILE)) >= 31
        flag = lambda chosen: jnp.where(chosen, 1.0, 0.0).astype(F32)
        active = flag(first & (count > 0)) + flag(second & (count > 1))
        mask[0:1, :] = flag(first)
        mask[1:2, :] = flag(second)
        mask[2:3, :] = jnp.where(last, 0.0, active)
        mask[3:8, :] = jnp.zeros((5, TILE), F32)
        send(mask, mask_in, edge_sems, 0, me.region_by(1))

    def edge_start():
        await_bytes(mask_in, edge_recv.at[0])
        for plane in range(2):
            up[plane] = mid[plane, :EDGE] + dual(0, plane)
            low[plane] = mid[plane, TILE - EDGE:] + dual(1, plane)
            up_sent[plane] = packed(up[plane], mask_in)
            low_sent[plane] = packed(low[plane], mask)

    def edge_send_plane(plane):
        send(up_sent.at[plane], from_below.at[plane], edge_sems, 1 + plane, me.region_by(-1))
        send(low_sent.at[plane], from_above.at[plane], edge_sems, 3 + plane, me.region_by(1))

    def edge_end():
        for plane in range(2):
            await_bytes(from_below.at[plane], edge_recv.at[1 + plane])
            await_bytes(from_above.at[plane], edge_recv.at[3 + plane])
            here = mid[plane, TILE - EDGE:]
            agreed = 0.5 * (low[plane] + unpacked(from_below[plane], mask))
            active = jnp.broadcast_to(mask[2:3, :], (EDGE, TILE)) > 0.5
            bottom_out[plane] = jnp.where(active, dual(1, plane) + (here - agreed), dual(1, plane))
            mid[plane, TILE - EDGE:] = jnp.where(active, agreed, here)
            here = mid[plane, :EDGE]
            agreed = 0.5 * (unpacked(from_above[plane], mask_in) + up[plane])
            active = jnp.broadcast_to(mask_in[2:3, :], (EDGE, TILE)) > 0.5
            top_out[plane] = jnp.where(active, dual(0, plane) + (here - agreed), dual(0, plane))
            mid[plane, :EDGE] = jnp.where(active, agreed, here)

    wait_loads(0, 10)
    wait_loads(15, 16)
    lax.fori_loop(0, 1, forward, 0)
    wait_loads(10, 15)
    wait_loads(16, 19)
    denom[...] = work[POWER:POWER + PAT, :PAT]
    lax.fori_loop(1, 2, forward, 0)
    lax.fori_loop(2, 3, forward, 0)
    pl.semaphore_wait(barrier, 21)
    mask_start()
    core_start(MODES)
    lax.fori_loop(3, 4, forward, 0)
    line_start(MODES)
    inverse(0, 0, 4)
    core_start(0)
    inverse(1, 0, 2)
    line_start(0)
    plane_start(MODES)
    inverse(1, 2, 4)
    core_start(1)
    inverse(2, 0, 2)
    line_start(1)
    inverse(2, 2, 4)
    core_start(2)
    plane_start(0)
    inverse(3, 0, 2)
    line_start(2)
    inverse(3, 2, 4)
    core_start(3)
    spread(0, 2)
    plane_start(1)
    line_start(3)
    spread(2, 4)
    denom_end()
    back_start(0)
    plane_start(2)
    spread_weights()
    wait_loads(19, LOADS)
    update((0, TILE - EDGE), EDGE)
    plane_start(3)
    edge_start()
    edge_send_plane(0)
    update((EDGE,), TILE // 2 - EDGE)
    back_start(1)
    back_line_start(0)
    update((TILE // 2,), TILE // 2 - EDGE)
    back_start(2)
    back_start(3)
    edge_send_plane(1)
    back_line_start(1)
    back_core_start(0)
    back_line_start(2)
    back_line_start(3)
    back_core_start(1)
    edge_end()
    back_core_start(2)
    back_end(0)
    back_core_start(3)
    back_end(1)
    back_end(2)
    back_end(3)

    for m in range(SUMS):
        await_bytes(from_core.at[m], core_send.at[m])
        await_bytes(from_line.at[m], line_send.at[m])
        await_bytes(from_plane.at[m], plane_send.at[m])
    for m in range(MODES):
        await_bytes(tiles.at[m, pl.ds(0, 15)], back_plane_send.at[m])
        await_bytes(fresh.at[0, m, pl.ds(0, 192), :], back_line_send.at[m])
        await_bytes(fresh.at[0, m], back_core_send.at[m])
    await_bytes(mask_in, edge_send.at[0])
    for plane in range(2):
        await_bytes(up_sent.at[plane], edge_send.at[1 + plane])
        await_bytes(low_sent.at[plane], edge_send.at[3 + plane])


def write_out(mid, probe, top, bottom, mid_out, probe_out, top_out, bottom_out, sems):
    copies = []
    for plane in range(2):
        copies.append((top.at[plane], top_out.at[plane]))
        copies.append((bottom.at[plane], bottom_out.at[plane]))
        for i in range(2):
            rows = pl.ds(i * PAT, PAT)
            copies.append((mid.at[plane, rows], mid_out.at[plane, rows]))
            copies.append((probe.at[plane, pl.ds(2 * i, 2)], probe_out.at[plane, pl.ds(2 * i, 2)]))
    copies = [pltpu.make_async_copy(source, target, sems.at[i]) for i, (source, target) in enumerate(copies)]
    for copy in copies:
        copy.start()
    for copy in copies:
        copy.wait()


def local(object_field, probe, amplitudes, positions, dual_top, dual_bottom, pieces, live):
    tab = tables()
    vmem = pl.BlockSpec(memory_space=pltpu.VMEM)
    smem = pl.BlockSpec(memory_space=pltpu.SMEM)
    far = pl.BlockSpec(memory_space=pltpu.HBM)
    anywhere = pl.BlockSpec(memory_space=pl.ANY)
    buf = lambda *shape: pltpu.VMEM(shape, F32)
    half = lambda *shape: pltpu.VMEM(shape, BF16)
    dma = lambda *shape: pltpu.SemaphoreType.DMA(shape)
    edge, sent = (2, EDGE, TILE), (2, EDGE, KP * BLOCK)
    shape = lambda *dims: jax.ShapeDtypeStruct(dims, F32)
    prepared = pl.pallas_call(
        prepare,
        out_shape=shape(DUALS + PAT, TILE),
        in_specs=[smem] + [far] * 3,
        out_specs=far,
        scratch_shapes=[buf(DUALS + PAT, TILE), buf(2, TILE, TILE), dma(13)],
        compiler_params=pltpu.CompilerParams(vmem_limit_bytes=60 * 1024 * 1024),
    )(positions.T, object_field, dual_top, dual_bottom)
    results = pl.pallas_call(
        kernel,
        out_shape=(shape(2, TILE, TILE), shape(2, MODES, PAT, PAT), shape(*edge), shape(*edge)),
        in_specs=[far] * 3 + [vmem] * 2 + [far] * 2,
        out_specs=(vmem,) * 4,
        scratch_shapes=[
            buf(MODES * NPAT, 2, PAT, PAT), buf(NPAT, 2, PAT, PAT), buf(NPAT, 2, PAT, PAT),
            half(3, NPAT * PAT, TILE), half(3, NPAT * PAT, TILE), buf(2, MODES, PAT, PAT),
            buf(SUMS, PAT, PAT), buf(SUMS, PAT, PAT), buf(SUMS, 3, 64, PAT), buf(SUMS, 16, 8, HALF), buf(SUMS, 15, 8, HALF),
            buf(MODES, 16, 8, HALF), buf(2, MODES, PAT, PAT), buf(8, HALF),
            buf(DUALS + PAT, TILE), buf(PAT, PAT), buf(2, MODES, PAT, PAT), half(2, 2, 2, PAT, PAT), buf(2, TILE, TILE), buf(NPAT, PAT, PAT), half(2, PAT, PAT), buf(8, TILE), buf(8, TILE), buf(*edge), buf(*edge), buf(*sent), buf(*sent), buf(*sent), buf(*sent),
        ] + [dma(SUMS)] * 6 + [dma(MODES)] * 6 + [dma(5), dma(5), dma(LOADS)],
        compiler_params=pltpu.CompilerParams(vmem_limit_bytes=LIMIT * 1024 * 1024, collective_id=0, has_side_effects=True),
    )(prepared, probe, jnp.asarray(tab), pieces.T, live, object_field, amplitudes)
    return pl.pallas_call(
        write_out,
        out_shape=(shape(2, TILE, TILE), shape(2, MODES, PAT, PAT), shape(*edge), shape(*edge)),
        in_specs=[anywhere] * 4,
        out_specs=(far,) * 4,
        scratch_shapes=[dma(12)],
        compiler_params=pltpu.CompilerParams(vmem_limit_bytes=1024 * 1024),
    )(*results)


def solution(mesh):
    tiles = P(None, "region", "group")
    return jax.shard_map(
        local,
        mesh=mesh,
        in_specs=(tiles, P(), P("region", "group", None), P("region", "group"), tiles, tiles, P("region", "group"), P("region", "group")),
        out_specs=(tiles, P(), tiles, tiles),
        check_vma=False,
    )
```

```python
import numpy as np
import jax
import jax.numpy as jnp
import ml_dtypes
from jax import lax
from jax.experimental import pallas as pl
from jax.experimental.pallas import tpu as pltpu
from jax.sharding import PartitionSpec as P

F32, BF16 = jnp.float32, jnp.bfloat16
MESH = pl.DeviceIdType.MESH
PAT, TILE, MODES, NPAT, HALF = 256, 512, 4, 4, 128
EDGE, BLOCK, NPIECE, KP = 64, 128, 4, 2
LOADS = 21
LIMIT = 46
POWER, DUALS = NPAT * PAT, (NPAT + 1) * PAT
SUMS = MODES + 1


def tables():
    n = np.arange(HALF)[:, None]
    out = []
    for p in range(2):
        k = 2 * np.arange(HALF)[None, :] + p
        angle = 2 * np.pi * ((n * k) % PAT) / PAT
        c, s = np.cos(angle) / 16.0, np.sin(angle) / 16.0
        full = np.block([[c, -s], [s, c]])
        out.append(full)
    full = np.stack([np.stack(out), np.stack([o.T for o in out])]).astype(np.float32)
    hi = full.astype(ml_dtypes.bfloat16)
    lo = (full - hi.astype(np.float32)).astype(ml_dtypes.bfloat16)
    return np.stack([hi, lo], axis=2)


def dot(a, b):
    return jnp.dot(a, b, preferred_element_type=F32)


def split(a):
    h = a.astype(BF16)
    return h, (a - h.astype(F32)).astype(BF16)


def right_of(parts, t, d, p):
    h, l = parts
    return dot(h, t[d, p, 1]) + dot(h, t[d, p, 0]) + dot(l, t[d, p, 0])


def left_of(t, d, p, parts):
    h, l = parts
    return dot(t[d, p, 0], l) + dot(t[d, p, 1], h) + dot(t[d, p, 0], h)


def along(shape, axis):
    return lax.broadcasted_iota(jnp.int32, shape, axis)


def lane_turn(block, by):
    return pltpu.roll(block, by & (HALF - 1), 1)


def row_turn(block, by):
    return pltpu.roll(block, by & 7, 1)


def window(obj, plane, row, col):
    base = pl.multiple_of(jnp.minimum((row >> 3) << 3, TILE - PAT - 8), 8)
    side = pl.multiple_of(jnp.minimum((col >> 7) << 7, TILE - PAT - HALF), HALF)
    down, right_by = row - base, col - side
    block = obj[plane, pl.ds(base, PAT + 8), pl.ds(side, PAT + HALF)]
    block = block.reshape((PAT + 8) // 8, 8, PAT + HALF)
    turned = row_turn(block, 8 - down)
    keep = along((PAT // 8, 8, PAT + HALF), 1) + down < 8
    block = jnp.where(keep, turned[:-1], turned[1:]).reshape(PAT, PAT + HALF)
    parts = [lane_turn(block[:, t * HALF:(t + 1) * HALF], HALF - right_by) for t in range(3)]
    keep = along((PAT, HALF), 1) + right_by < HALF
    return jnp.concatenate([jnp.where(keep, parts[t], parts[t + 1]) for t in range(2)], axis=1)


def prepare(pos, far_obj, far_top, far_bottom, work_out, work, obj, sems):
    loads, stores = [], []
    for i in range(4):
        rows = (i // 2, pl.ds((i % 2) * PAT, PAT))
        loads.append(pltpu.make_async_copy(far_obj.at[rows], obj.at[rows], sems.at[i]))
    for i, source in enumerate((far_top.at[0], far_top.at[1], far_bottom.at[0], far_bottom.at[1])):
        loads.append(pltpu.make_async_copy(source, work.at[pl.ds(DUALS + i * EDGE, EDGE)], sems.at[4 + i]))
    for copy in loads:
        copy.start()
    for j in range(NPAT):
        work[POWER + j:POWER + j + 1, PAT:] = jnp.full((1, PAT), pos[0, j].astype(F32), F32)
        work[POWER + NPAT + j:POWER + NPAT + j + 1, PAT:] = jnp.full((1, PAT), pos[1, j].astype(F32), F32)
    for copy in loads[:4]:
        copy.wait()
    total = jnp.zeros((PAT, PAT), F32)
    for j in range(NPAT):
        pr, pi = window(obj, 0, pos[0, j], pos[1, j]), window(obj, 1, pos[0, j], pos[1, j])
        rows = pl.ds(j * PAT, PAT)
        work[rows, :PAT] = pr
        work[rows, PAT:] = pi
        stores.append(pltpu.make_async_copy(work.at[rows], work_out.at[rows], sems.at[8 + j]))
        stores[-1].start()
        total = total + pr * pr + pi * pi
    work[POWER:POWER + PAT, :PAT] = total
    for copy in loads[4:]:
        copy.wait()
    rows = pl.ds(POWER, 2 * PAT)
    stores.append(pltpu.make_async_copy(work.at[rows], work_out.at[rows], sems.at[12]))
    stores[-1].start()
    for copy in stores:
        copy.wait()


class Place:
    def __init__(self):
        self.group, self.region = lax.axis_index("group"), lax.axis_index("region")
        core, y_lo = lax.rem(self.group, 2), self.group // 2
        x, z, y_hi = self.region // 8, lax.rem(self.region // 2, 4), lax.rem(self.region, 2)
        y = y_hi * 2 + y_lo
        self.core = core
        self.v, self.u, self.w = x + core * (z - x), y + core * (x - y), z + core * (y - z)
        self.number = self.u * 4 + self.w

    def at(self, v, u, w):
        core = self.core
        x, y, z = v + core * (u - v), u + core * (w - u), w + core * (v - w)
        return (lax.rem(y, 2) * 2 + core, (x * 4 + z) * 2 + y // 2)

    def sibling(self):
        return (self.group + 1 - 2 * self.core, self.region)

    def on_line(self, k):
        v = lax.rem(self.v + k, 4)
        return self.at(v, self.u, self.w), v

    def in_plane(self, k):
        u, w = lax.rem(self.u + k // 4, 4), lax.rem(self.w + lax.rem(k, 4), 4)
        return self.at(self.v, u, w), u * 4 + w

    def region_by(self, by):
        return (self.group, lax.rem(self.region + 32 + by, 32))


def send(src, dst, sems, index, device):
    copy = pltpu.make_async_remote_copy(
        src_ref=src, dst_ref=dst, send_sem=sems[0].at[index], recv_sem=sems[1].at[index], device_id=device, device_id_type=MESH
    )
    copy.start()


def await_bytes(ref, sem):
    pltpu.make_async_copy(ref, ref, sem).wait()


def packed(block, hot):
    out = []
    for slot in range(KP):
        chosen = block[:, :BLOCK]
        for b in range(1, NPIECE):
            flag = jnp.broadcast_to(hot[slot:slot + 1, b * BLOCK:(b + 1) * BLOCK], chosen.shape)
            chosen = jnp.where(flag > 0.5, block[:, b * BLOCK:(b + 1) * BLOCK], chosen)
        out.append(chosen)
    return jnp.concatenate(out, axis=1)


def unpacked(block, hot):
    flag = jnp.broadcast_to(hot[0:1, :], (block.shape[0], TILE)) > 0.5
    first = jnp.concatenate([block[:, :BLOCK]] * NPIECE, axis=1)
    second = jnp.concatenate([block[:, BLOCK:]] * NPIECE, axis=1)
    return jnp.where(flag, first, second)


def kernel(
    far_work, far_probe, far_tab, pieces, live, far_obj, far_amp,
    mid, probe_out, top_out, bottom_out,
    far, factor, spread_hi, spread_lo, numer,
    from_core, part, from_line, block, from_plane, tiles, fresh, scale,
    work, denom, probe, tab, obj, amp, perm, mask, mask_in, up, low, up_sent, low_sent, from_below, from_above,
    core_send, core_recv, line_send, line_recv, plane_send, plane_recv,
    back_plane_send, back_plane_recv, back_line_send, back_line_recv, back_core_send, back_core_recv,
    edge_send, edge_recv, load_sem,
):
    pairs = [(far_work.at[pl.ds(j * PAT, PAT)], work.at[pl.ds(j * PAT, PAT)]) for j in range(NPAT + 2)]
    pairs = [(far_tab, tab)] + [(far_probe.at[plane, m], probe.at[plane, m]) for m in range(MODES) for plane in range(2)] + pairs
    pairs += [(far_amp.at[j], amp.at[j]) for j in range(NPAT)] + [(far_obj.at[plane], obj.at[plane]) for plane in range(2)]
    loads = [pltpu.make_async_copy(source, target, load_sem.at[i]) for i, (source, target) in enumerate(pairs)]
    for load in loads:
        load.start()

    def wait_loads(first, last):
        for load in loads[first:last]:
            load.wait()

    me = Place()
    barrier = pltpu.get_barrier_semaphore()

    def greet(device):
        pl.semaphore_signal(barrier, inc=1, device_id=device, device_id_type=MESH)

    greet(me.sibling())
    for k in range(1, 4):
        greet(me.on_line(k)[0])
    for k in range(1, 16):
        greet(me.in_plane(k)[0])
    greet(me.region_by(1))
    greet(me.region_by(-1))

    for i, (axis, other) in enumerate(((1, 0), (0, 1))):
        place = along((PAT, PAT), axis)
        source = 2 * (place & (HALF - 1)) + (place >> 7)
        perm[i] = jnp.where(along((PAT, PAT), other) == source, 1.0, 0.0).astype(BF16)
    def window_of(j):
        rows = pl.ds(pl.multiple_of(j * PAT, PAT), PAT)
        return work[rows, :PAT], work[rows, PAT:]

    def forward(j):
        def exit_of(m):
            pr, pi = window_of(j)
            qr, qi = probe[0, m], probe[1, m]
            er = qr * pr - qi * pi
            ei = qr * pi + qi * pr
            lo = jnp.concatenate([er[:, :HALF], ei[:, :HALF]], axis=1)
            hi = jnp.concatenate([er[:, HALF:], ei[:, HALF:]], axis=1)
            return split(lo + hi), split(lo - hi)

        def first_of(parts):
            y0 = right_of(parts[0], tab, 0, 0)
            y1 = right_of(parts[1], tab, 0, 1)
            yr = jnp.concatenate([y0[:, :HALF], y1[:, :HALF]], axis=1)
            yi = jnp.concatenate([y0[:, HALF:], y1[:, HALF:]], axis=1)
            top = jnp.concatenate([yr[:HALF], yi[:HALF]], axis=0)
            bot = jnp.concatenate([yr[HALF:], yi[HALF:]], axis=0)
            return split(top + bot), split(top - bot)

        def second_of(m, parts):
            far[m * NPAT + j, 0] = left_of(tab, 1, 0, parts[0])
            far[m * NPAT + j, 1] = left_of(tab, 1, 1, parts[1])

        exits = [exit_of(m) for m in range(MODES)]
        halfway = [first_of(parts) for parts in exits]
        for m in range(MODES):
            second_of(m, halfway[m])
        h, l = split(amp[j])
        h, l = split(dot(h, perm[0]) + dot(l, perm[0]))
        full = dot(perm[1], h) + dot(perm[1], l)
        for q in range(2):
            power = jnp.zeros((HALF, PAT), F32)
            for m in range(MODES):
                z = far[m * NPAT + j, q]
                power = power + z[:HALF] * z[:HALF] + z[HALF:] * z[HALF:]
            f = full[q * HALF:(q + 1) * HALF] / jnp.maximum(jnp.sqrt(power), 0.5)
            factor[j, q, :HALF] = f
            factor[j, q, HALF:] = f

    def inverse(m, first, last):
        positions = range(first, last)

        def fixed_of(j):
            return split(far[m * NPAT + j, 0] * factor[j, 0]), split(far[m * NPAT + j, 1] * factor[j, 1])

        def first_of(parts):
            g0 = left_of(tab, 0, 0, parts[0])
            g1 = left_of(tab, 0, 1, parts[1])
            top, bot = g0 + g1, g0 - g1
            xr = jnp.concatenate([top[:HALF], bot[:HALF]], axis=0)
            xi = jnp.concatenate([top[HALF:], bot[HALF:]], axis=0)
            a0 = jnp.concatenate([xr[:, :HALF], xi[:, :HALF]], axis=1)
            a1 = jnp.concatenate([xr[:, HALF:], xi[:, HALF:]], axis=1)
            return split(a0), split(a1)

        def back_of(j, parts):
            b0 = right_of(parts[0], tab, 1, 0)
            b1 = right_of(parts[1], tab, 1, 1)
            lo, hi = b0 + b1, b0 - b1
            br = jnp.concatenate([lo[:, :HALF], hi[:, :HALF]], axis=1)
            bi = jnp.concatenate([lo[:, HALF:], hi[:, HALF:]], axis=1)
            far[m * NPAT + j, 0] = br
            far[m * NPAT + j, 1] = bi
            pr, pi = window_of(j)
            real, imag = pr * br + pi * bi, pr * bi - pi * br
            numer[0, m] = real if j == 0 else numer[0, m] + real
            numer[1, m] = imag if j == 0 else numer[1, m] + imag

        fixed = [fixed_of(j) for j in positions]
        halfway = [first_of(parts) for parts in fixed]
        for j, parts in zip(positions, halfway):
            back_of(j, parts)

    line_rows = pl.ds(pl.multiple_of(me.v * 64, 64), 64)
    core_sems, line_sems, plane_sems = (core_send, core_recv), (line_send, line_recv), (plane_send, plane_recv)
    back_plane_sems, back_line_sems = (back_plane_send, back_plane_recv), (back_line_send, back_line_recv)
    back_core_sems, edge_sems = (back_core_send, back_core_recv), (edge_send, edge_recv)

    def mine(m):
        return denom[...] if m == MODES else numer[me.core, m]

    def core_start(m):
        send(denom if m == MODES else numer.at[1 - me.core, m], from_core.at[m], core_sems, m, me.sibling())

    def line_start(m):
        await_bytes(from_core.at[m], core_recv.at[m])
        part[m] = mine(m) + from_core[m]
        for k in range(1, 4):
            device, there = me.on_line(k)
            source = part.at[m, pl.ds(pl.multiple_of(there * 64, 64), 64), :]
            send(source, from_line.at[m, k - 1], line_sems, m, device)

    def plane_start(m):
        await_bytes(from_line.at[m], line_recv.at[m])
        total = part[m, line_rows, :] + from_line[m, 0] + from_line[m, 1] + from_line[m, 2]
        for k in range(16):
            block[m, k] = total[(k // 2) * 8:(k // 2) * 8 + 8, (k % 2) * HALF:(k % 2 + 1) * HALF]

        for k in range(1, 16):
            device, there = me.in_plane(k)
            send(block.at[m, there], from_plane.at[m, k - 1], plane_sems, m, device)

    def total_of(m):
        await_bytes(from_plane.at[m], plane_recv.at[m])
        total = block[m, me.number]
        for k in range(15):
            total = total + from_plane[m, k]
        return total

    def denom_end():
        scale[...] = total_of(MODES) + 1.0

    def back_start(m):
        row = pl.multiple_of(me.v * 64 + (me.number // 2) * 8, 8)
        column = pl.multiple_of(lax.rem(me.number, 2) * HALF, HALF)
        old = probe[me.core, m, pl.ds(row, 8), pl.ds(column, HALF)]
        tiles[m, me.number] = (old + total_of(m)) / scale[...]
        own = tiles.at[m, me.number]

        for k in range(1, 16):
            send(own, own, back_plane_sems, m, me.in_plane(k)[0])

    def back_line_start(m):
        await_bytes(tiles.at[m, pl.ds(0, 15)], back_plane_recv.at[m])
        rows = [jnp.concatenate([tiles[m, 2 * i], tiles[m, 2 * i + 1]], axis=1) for i in range(8)]
        fresh[me.core, m, line_rows, :] = jnp.concatenate(rows, axis=0)
        own = fresh.at[me.core, m, line_rows, :]
        for k in range(1, 4):
            send(own, own, back_line_sems, m, me.on_line(k)[0])

    def back_core_start(m):
        await_bytes(fresh.at[me.core, m, pl.ds(0, 192), :], back_line_recv.at[m])
        send(fresh.at[me.core, m], fresh.at[me.core, m], back_core_sems, m, me.sibling())

    def back_end(m):
        await_bytes(fresh.at[1 - me.core, m], back_core_recv.at[m])
        for plane in range(2):
            probe_out[plane, m] = fresh[plane, m]

    def spread_plane(plane, j, block):
        rows = pl.ds(pl.multiple_of(j * PAT, PAT), PAT)
        by = jnp.broadcast_to(work[pl.ds(POWER + NPAT + j, 1), PAT:], (PAT, PAT)).astype(jnp.int32)
        by = jnp.concatenate([by, by], axis=1)
        columns = jnp.where(along((PAT, TILE), 1) - along((PAT, TILE), 0) == by, 1.0, 0.0).astype(BF16)
        h, l = split(block)
        h, l = split(dot(h, columns) + dot(l, columns))
        spread_hi[plane, rows, :] = h
        spread_lo[plane, rows, :] = l

    def spread(first, last):
        def one(j, _):
            real, imag = jnp.zeros((PAT, PAT), F32), jnp.zeros((PAT, PAT), F32)
            for m in range(MODES):
                br, bi, qr, qi = far[m * NPAT + j, 0], far[m * NPAT + j, 1], probe[0, m], probe[1, m]
                real = real + qr * br + qi * bi
                imag = imag + qr * bi - qi * br
            spread_plane(0, j, real)
            spread_plane(1, j, imag)
            return 0

        lax.fori_loop(first, last, one, 0, unroll=True)

    def spread_weights():
        power = sum(probe[0, m] * probe[0, m] + probe[1, m] * probe[1, m] for m in range(MODES))
        for j in range(NPAT):
            spread_plane(2, j, power)

    def update(starts, count):
        chosen = []
        for j in range(NPAT):
            by = jnp.broadcast_to(work[POWER + j:POWER + j + 1, PAT:], (count, PAT)).astype(jnp.int32)
            away = along((count, PAT), 0) - along((count, PAT), 1)
            chosen.append(jnp.concatenate([jnp.where(away + start == by, 1.0, 0.0).astype(BF16) for start in starts], axis=0))
        chosen = jnp.concatenate(chosen, axis=1)
        sums = [dot(chosen, spread_hi[plane]) + dot(chosen, spread_lo[plane]) for plane in range(3)]
        for i, start in enumerate(starts):
            rows, here = slice(start, start + count), slice(i * count, (i + 1) * count)
            inverse_weight = 1.0 / (sums[2][here] + 1.0)
            for plane in range(2):
                mid[plane, rows, :] = (obj[plane, rows, :] + sums[plane][here]) * inverse_weight

    def dual(side, plane):
        start = DUALS + (2 * side + plane) * EDGE
        return work[start:start + EDGE, :]

    def mask_start():
        wide = lambda ref, i: jnp.broadcast_to(ref[0:1, i:i + 1], (1, TILE))
        number = along((1, TILE), 1) // BLOCK
        first, second, count = wide(pieces, 0) == number, wide(pieces, 1) == number, wide(live, 0)
        last = jnp.broadcast_to(me.region, (1, TILE)) >= 31
        flag = lambda chosen: jnp.where(chosen, 1.0, 0.0).astype(F32)
        active = flag(first & (count > 0)) + flag(second & (count > 1))
        mask[0:1, :] = flag(first)
        mask[1:2, :] = flag(second)
        mask[2:3, :] = jnp.where(last, 0.0, active)
        mask[3:8, :] = jnp.zeros((5, TILE), F32)
        send(mask, mask_in, edge_sems, 0, me.region_by(1))

    def edge_start():
        await_bytes(mask_in, edge_recv.at[0])
        for plane in range(2):
            up[plane] = mid[plane, :EDGE] + dual(0, plane)
            low[plane] = mid[plane, TILE - EDGE:] + dual(1, plane)
            up_sent[plane] = packed(up[plane], mask_in)
            low_sent[plane] = packed(low[plane], mask)

    def edge_send_plane(plane):
        send(up_sent.at[plane], from_below.at[plane], edge_sems, 1 + plane, me.region_by(-1))
        send(low_sent.at[plane], from_above.at[plane], edge_sems, 3 + plane, me.region_by(1))

    def edge_end():
        for plane in range(2):
            await_bytes(from_below.at[plane], edge_recv.at[1 + plane])
            await_bytes(from_above.at[plane], edge_recv.at[3 + plane])
            here = mid[plane, TILE - EDGE:]
            agreed = 0.5 * (low[plane] + unpacked(from_below[plane], mask))
            active = jnp.broadcast_to(mask[2:3, :], (EDGE, TILE)) > 0.5
            bottom_out[plane] = jnp.where(active, dual(1, plane) + (here - agreed), dual(1, plane))
            mid[plane, TILE - EDGE:] = jnp.where(active, agreed, here)
            here = mid[plane, :EDGE]
            agreed = 0.5 * (unpacked(from_above[plane], mask_in) + up[plane])
            active = jnp.broadcast_to(mask_in[2:3, :], (EDGE, TILE)) > 0.5
            top_out[plane] = jnp.where(active, dual(0, plane) + (here - agreed), dual(0, plane))
            mid[plane, :EDGE] = jnp.where(active, agreed, here)

    wait_loads(0, 10)
    wait_loads(15, 16)
    forward(0)
    wait_loads(10, 15)
    wait_loads(16, 19)
    denom[...] = work[POWER:POWER + PAT, :PAT]
    forward(1)
    forward(2)
    pl.semaphore_wait(barrier, 21)
    mask_start()
    core_start(MODES)
    forward(3)
    line_start(MODES)
    inverse(0, 0, 4)
    core_start(0)
    inverse(1, 0, 2)
    line_start(0)
    inverse(1, 2, 4)
    core_start(1)
    plane_start(MODES)
    inverse(2, 0, 2)
    line_start(1)
    inverse(2, 2, 4)
    core_start(2)
    inverse(3, 0, 2)
    plane_start(0)
    line_start(2)
    inverse(3, 2, 4)
    core_start(3)
    spread(0, 1)
    line_start(3)
    plane_start(1)
    denom_end()
    spread(1, 2)
    spread(2, 4)
    back_start(0)
    plane_start(2)
    spread_weights()
    wait_loads(19, LOADS)
    update((0, TILE - EDGE), EDGE)
    edge_start()
    plane_start(3)
    back_start(1)
    update((EDGE,), TILE // 2 - EDGE)
    back_line_start(0)
    back_start(2)
    update((TILE // 2,), TILE // 2 - EDGE)
    back_start(3)
    edge_send_plane(0)
    back_line_start(1)
    back_core_start(0)
    back_line_start(2)
    back_line_start(3)
    edge_send_plane(1)
    back_core_start(1)
    back_core_start(2)
    back_end(0)
    back_core_start(3)
    back_end(1)
    back_end(2)
    edge_end()
    back_end(3)

    for m in range(SUMS):
        await_bytes(from_core.at[m], core_send.at[m])
        await_bytes(from_line.at[m], line_send.at[m])
        await_bytes(from_plane.at[m], plane_send.at[m])
    for m in range(MODES):
        await_bytes(tiles.at[m, pl.ds(0, 15)], back_plane_send.at[m])
        await_bytes(fresh.at[0, m, pl.ds(0, 192), :], back_line_send.at[m])
        await_bytes(fresh.at[0, m], back_core_send.at[m])
    await_bytes(mask_in, edge_send.at[0])
    for plane in range(2):
        await_bytes(up_sent.at[plane], edge_send.at[1 + plane])
        await_bytes(low_sent.at[plane], edge_send.at[3 + plane])


def write_out(mid, probe, top, bottom, mid_out, probe_out, top_out, bottom_out, sems):
    copies = []
    for plane in range(2):
        copies.append((top.at[plane], top_out.at[plane]))
        copies.append((bottom.at[plane], bottom_out.at[plane]))
        for i in range(2):
            rows = pl.ds(i * PAT, PAT)
            copies.append((mid.at[plane, rows], mid_out.at[plane, rows]))
            copies.append((probe.at[plane, pl.ds(2 * i, 2)], probe_out.at[plane, pl.ds(2 * i, 2)]))
    copies = [pltpu.make_async_copy(source, target, sems.at[i]) for i, (source, target) in enumerate(copies)]
    for copy in copies:
        copy.start()
    for copy in copies:
        copy.wait()


def local(object_field, probe, amplitudes, positions, dual_top, dual_bottom, pieces, live):
    tab = tables()
    vmem = pl.BlockSpec(memory_space=pltpu.VMEM)
    smem = pl.BlockSpec(memory_space=pltpu.SMEM)
    far = pl.BlockSpec(memory_space=pltpu.HBM)
    anywhere = pl.BlockSpec(memory_space=pl.ANY)
    buf = lambda *shape: pltpu.VMEM(shape, F32)
    half = lambda *shape: pltpu.VMEM(shape, BF16)
    dma = lambda *shape: pltpu.SemaphoreType.DMA(shape)
    edge, sent = (2, EDGE, TILE), (2, EDGE, KP * BLOCK)
    shape = lambda *dims: jax.ShapeDtypeStruct(dims, F32)
    prepared = pl.pallas_call(
        prepare,
        out_shape=shape(DUALS + PAT, TILE),
        in_specs=[smem] + [far] * 3,
        out_specs=far,
        scratch_shapes=[buf(DUALS + PAT, TILE), buf(2, TILE, TILE), dma(13)],
        compiler_params=pltpu.CompilerParams(vmem_limit_bytes=60 * 1024 * 1024),
    )(positions.T, object_field, dual_top, dual_bottom)
    results = pl.pallas_call(
        kernel,
        out_shape=(shape(2, TILE, TILE), shape(2, MODES, PAT, PAT), shape(*edge), shape(*edge)),
        in_specs=[far] * 3 + [vmem] * 2 + [far] * 2,
        out_specs=(vmem,) * 4,
        scratch_shapes=[
            buf(MODES * NPAT, 2, PAT, PAT), buf(NPAT, 2, PAT, PAT),
            half(3, NPAT * PAT, TILE), half(3, NPAT * PAT, TILE), buf(2, MODES, PAT, PAT),
            buf(SUMS, PAT, PAT), buf(SUMS, PAT, PAT), buf(SUMS, 3, 64, PAT), buf(SUMS, 16, 8, HALF), buf(SUMS, 15, 8, HALF),
            buf(MODES, 16, 8, HALF), buf(2, MODES, PAT, PAT), buf(8, HALF),
            buf(DUALS + PAT, TILE), buf(PAT, PAT), buf(2, MODES, PAT, PAT), half(2, 2, 2, PAT, PAT), buf(2, TILE, TILE), buf(NPAT, PAT, PAT), half(2, PAT, PAT), buf(8, TILE), buf(8, TILE), buf(*edge), buf(*edge), buf(*sent), buf(*sent), buf(*sent), buf(*sent),
        ] + [dma(SUMS)] * 6 + [dma(MODES)] * 6 + [dma(5), dma(5), dma(LOADS)],
        compiler_params=pltpu.CompilerParams(vmem_limit_bytes=LIMIT * 1024 * 1024, collective_id=0, has_side_effects=True),
    )(prepared, probe, jnp.asarray(tab), pieces.T, live, object_field, amplitudes)
    return pl.pallas_call(
        write_out,
        out_shape=(shape(2, TILE, TILE), shape(2, MODES, PAT, PAT), shape(*edge), shape(*edge)),
        in_specs=[anywhere] * 4,
        out_specs=(far,) * 4,
        scratch_shapes=[dma(12)],
        compiler_params=pltpu.CompilerParams(vmem_limit_bytes=1024 * 1024),
    )(*results)


def solution(mesh):
    tiles = P(None, "region", "group")
    return jax.shard_map(
        local,
        mesh=mesh,
        in_specs=(tiles, P(), P("region", "group", None), P("region", "group"), tiles, tiles, P("region", "group"), P("region", "group")),
        out_specs=(tiles, P(), tiles, tiles),
        check_vma=False,
    )
```

```python
import numpy as np
import jax
import jax.numpy as jnp
import ml_dtypes
from jax import lax
from jax.experimental import pallas as pl
from jax.experimental.pallas import tpu as pltpu
from jax.sharding import PartitionSpec as P

F32, BF16 = jnp.float32, jnp.bfloat16
MESH = pl.DeviceIdType.MESH
PAT, TILE, MODES, NPAT, HALF = 256, 512, 4, 4, 128
EDGE, BLOCK, NPIECE, KP = 64, 128, 4, 2
LOADS = 21
LIMIT = 46
POWER, DUALS = NPAT * PAT, (NPAT + 1) * PAT
SUMS = MODES + 1


def tables():
    n = np.arange(HALF)[:, None]
    out = []
    for p in range(2):
        k = 2 * np.arange(HALF)[None, :] + p
        angle = 2 * np.pi * ((n * k) % PAT) / PAT
        c, s = np.cos(angle) / 16.0, np.sin(angle) / 16.0
        full = np.block([[c, -s], [s, c]])
        out.append(full)
    full = np.stack([np.stack(out), np.stack([o.T for o in out])]).astype(np.float32)
    hi = full.astype(ml_dtypes.bfloat16)
    lo = (full - hi.astype(np.float32)).astype(ml_dtypes.bfloat16)
    return np.stack([hi, lo], axis=2)


def dot(a, b):
    return jnp.dot(a, b, preferred_element_type=F32)


def split(a):
    h = a.astype(BF16)
    return h, (a - h.astype(F32)).astype(BF16)


def right_of(parts, t, d, p):
    h, l = parts
    return dot(h, t[d, p, 1]) + dot(h, t[d, p, 0]) + dot(l, t[d, p, 0])


def left_of(t, d, p, parts):
    h, l = parts
    return dot(t[d, p, 0], l) + dot(t[d, p, 1], h) + dot(t[d, p, 0], h)


def along(shape, axis):
    return lax.broadcasted_iota(jnp.int32, shape, axis)


def lane_turn(block, by):
    return pltpu.roll(block, by & (HALF - 1), 1)


def row_turn(block, by):
    return pltpu.roll(block, by & 7, 1)


def window(obj, plane, row, col):
    base = pl.multiple_of(jnp.minimum((row >> 3) << 3, TILE - PAT - 8), 8)
    side = pl.multiple_of(jnp.minimum((col >> 7) << 7, TILE - PAT - HALF), HALF)
    down, right_by = row - base, col - side
    block = obj[plane, pl.ds(base, PAT + 8), pl.ds(side, PAT + HALF)]
    block = block.reshape((PAT + 8) // 8, 8, PAT + HALF)
    turned = row_turn(block, 8 - down)
    keep = along((PAT // 8, 8, PAT + HALF), 1) + down < 8
    block = jnp.where(keep, turned[:-1], turned[1:]).reshape(PAT, PAT + HALF)
    parts = [lane_turn(block[:, t * HALF:(t + 1) * HALF], HALF - right_by) for t in range(3)]
    keep = along((PAT, HALF), 1) + right_by < HALF
    return jnp.concatenate([jnp.where(keep, parts[t], parts[t + 1]) for t in range(2)], axis=1)


def prepare(pos, far_obj, far_top, far_bottom, work_out, work, obj, sems):
    loads, stores = [], []
    for i in range(4):
        rows = (i // 2, pl.ds((i % 2) * PAT, PAT))
        loads.append(pltpu.make_async_copy(far_obj.at[rows], obj.at[rows], sems.at[i]))
    for i, source in enumerate((far_top.at[0], far_top.at[1], far_bottom.at[0], far_bottom.at[1])):
        loads.append(pltpu.make_async_copy(source, work.at[pl.ds(DUALS + i * EDGE, EDGE)], sems.at[4 + i]))
    for copy in loads:
        copy.start()
    for j in range(NPAT):
        work[POWER + j:POWER + j + 1, PAT:] = jnp.full((1, PAT), pos[0, j].astype(F32), F32)
        work[POWER + NPAT + j:POWER + NPAT + j + 1, PAT:] = jnp.full((1, PAT), pos[1, j].astype(F32), F32)
    for copy in loads:
        copy.wait()
    rows = pl.ds(DUALS, PAT)
    stores.append(pltpu.make_async_copy(work.at[rows], work_out.at[rows], sems.at[13]))
    stores[-1].start()
    total = jnp.zeros((PAT, PAT), F32)
    for j in range(NPAT):
        pr, pi = window(obj, 0, pos[0, j], pos[1, j]), window(obj, 1, pos[0, j], pos[1, j])
        rows = pl.ds(j * PAT, PAT)
        work[rows, :PAT] = pr
        work[rows, PAT:] = pi
        stores.append(pltpu.make_async_copy(work.at[rows], work_out.at[rows], sems.at[8 + j]))
        stores[-1].start()
        total = total + pr * pr + pi * pi
    work[POWER:POWER + PAT, :PAT] = total
    rows = pl.ds(POWER, PAT)
    stores.append(pltpu.make_async_copy(work.at[rows], work_out.at[rows], sems.at[12]))
    stores[-1].start()
    for copy in stores:
        copy.wait()


class Place:
    def __init__(self):
        self.group, self.region = lax.axis_index("group"), lax.axis_index("region")
        core, y_lo = lax.rem(self.group, 2), self.group // 2
        x, z, y_hi = self.region // 8, lax.rem(self.region // 2, 4), lax.rem(self.region, 2)
        y = y_hi * 2 + y_lo
        self.core = core
        self.v, self.u, self.w = x + core * (z - x), y + core * (x - y), z + core * (y - z)
        self.number = self.u * 4 + self.w

    def at(self, v, u, w):
        core = self.core
        x, y, z = v + core * (u - v), u + core * (w - u), w + core * (v - w)
        return (lax.rem(y, 2) * 2 + core, (x * 4 + z) * 2 + y // 2)

    def sibling(self):
        return (self.group + 1 - 2 * self.core, self.region)

    def on_line(self, k):
        v = lax.rem(self.v + k, 4)
        return self.at(v, self.u, self.w), v

    def in_plane(self, k):
        u, w = lax.rem(self.u + k // 4, 4), lax.rem(self.w + lax.rem(k, 4), 4)
        return self.at(self.v, u, w), u * 4 + w

    def region_by(self, by):
        return (self.group, lax.rem(self.region + 32 + by, 32))


def send(src, dst, sems, index, device):
    copy = pltpu.make_async_remote_copy(
        src_ref=src, dst_ref=dst, send_sem=sems[0].at[index], recv_sem=sems[1].at[index], device_id=device, device_id_type=MESH
    )
    copy.start()


def await_bytes(ref, sem):
    pltpu.make_async_copy(ref, ref, sem).wait()


def packed(block, hot):
    out = []
    for slot in range(KP):
        chosen = block[:, :BLOCK]
        for b in range(1, NPIECE):
            flag = jnp.broadcast_to(hot[slot:slot + 1, b * BLOCK:(b + 1) * BLOCK], chosen.shape)
            chosen = jnp.where(flag > 0.5, block[:, b * BLOCK:(b + 1) * BLOCK], chosen)
        out.append(chosen)
    return jnp.concatenate(out, axis=1)


def unpacked(block, hot):
    flag = jnp.broadcast_to(hot[0:1, :], (block.shape[0], TILE)) > 0.5
    first = jnp.concatenate([block[:, :BLOCK]] * NPIECE, axis=1)
    second = jnp.concatenate([block[:, BLOCK:]] * NPIECE, axis=1)
    return jnp.where(flag, first, second)


def kernel(
    far_work, far_probe, far_tab, pieces, live, far_obj, far_amp,
    mid, probe_out, top_out, bottom_out,
    far, factor, spread_hi, spread_lo, numer,
    from_core, part, from_line, block, from_plane, tiles, fresh, scale,
    work, denom, probe, tab, obj, amp, perm, mask, mask_in, up, low, up_sent, low_sent, from_below, from_above,
    core_send, core_recv, line_send, line_recv, plane_send, plane_recv,
    back_plane_send, back_plane_recv, back_line_send, back_line_recv, back_core_send, back_core_recv,
    edge_send, edge_recv, load_sem,
):
    pairs = [(far_work.at[pl.ds(j * PAT, PAT)], work.at[pl.ds(j * PAT, PAT)]) for j in range(NPAT + 2)]
    pairs = [(far_tab, tab)] + [(far_probe.at[plane, m], probe.at[plane, m]) for m in range(MODES) for plane in range(2)] + pairs
    pairs += [(far_amp.at[j], amp.at[j]) for j in range(NPAT)] + [(far_obj.at[plane], obj.at[plane]) for plane in range(2)]
    loads = [pltpu.make_async_copy(source, target, load_sem.at[i]) for i, (source, target) in enumerate(pairs)]
    for load in loads:
        load.start()

    def wait_loads(first, last):
        for load in loads[first:last]:
            load.wait()

    me = Place()
    barrier = pltpu.get_barrier_semaphore()

    def greet(device):
        pl.semaphore_signal(barrier, inc=1, device_id=device, device_id_type=MESH)

    greet(me.sibling())
    for k in range(1, 4):
        greet(me.on_line(k)[0])
    for k in range(1, 16):
        greet(me.in_plane(k)[0])
    greet(me.region_by(1))
    greet(me.region_by(-1))

    for i, (axis, other) in enumerate(((1, 0), (0, 1))):
        place = along((PAT, PAT), axis)
        source = 2 * (place & (HALF - 1)) + (place >> 7)
        perm[i] = jnp.where(along((PAT, PAT), other) == source, 1.0, 0.0).astype(BF16)
    def window_of(j):
        rows = pl.ds(pl.multiple_of(j * PAT, PAT), PAT)
        return work[rows, :PAT], work[rows, PAT:]

    def forward(j):
        def exit_of(m):
            pr, pi = window_of(j)
            qr, qi = probe[0, m], probe[1, m]
            er = qr * pr - qi * pi
            ei = qr * pi + qi * pr
            lo = jnp.concatenate([er[:, :HALF], ei[:, :HALF]], axis=1)
            hi = jnp.concatenate([er[:, HALF:], ei[:, HALF:]], axis=1)
            return split(lo + hi), split(lo - hi)

        def first_of(parts):
            y0 = right_of(parts[0], tab, 0, 0)
            y1 = right_of(parts[1], tab, 0, 1)
            yr = jnp.concatenate([y0[:, :HALF], y1[:, :HALF]], axis=1)
            yi = jnp.concatenate([y0[:, HALF:], y1[:, HALF:]], axis=1)
            top = jnp.concatenate([yr[:HALF], yi[:HALF]], axis=0)
            bot = jnp.concatenate([yr[HALF:], yi[HALF:]], axis=0)
            return split(top + bot), split(top - bot)

        def second_of(m, parts):
            far[m * NPAT + j, 0] = left_of(tab, 1, 0, parts[0])
            far[m * NPAT + j, 1] = left_of(tab, 1, 1, parts[1])

        exits = [exit_of(m) for m in range(MODES)]
        halfway = [first_of(parts) for parts in exits]
        for m in range(MODES):
            second_of(m, halfway[m])
        h, l = split(amp[j])
        h, l = split(dot(h, perm[0]) + dot(l, perm[0]))
        full = dot(perm[1], h) + dot(perm[1], l)
        for q in range(2):
            power = jnp.zeros((HALF, PAT), F32)
            for m in range(MODES):
                z = far[m * NPAT + j, q]
                power = power + z[:HALF] * z[:HALF] + z[HALF:] * z[HALF:]
            f = full[q * HALF:(q + 1) * HALF] / jnp.maximum(jnp.sqrt(power), 0.5)
            factor[j, q, :HALF] = f
            factor[j, q, HALF:] = f

    def inverse(m, first, last):
        positions = range(first, last)

        def fixed_of(j):
            return split(far[m * NPAT + j, 0] * factor[j, 0]), split(far[m * NPAT + j, 1] * factor[j, 1])

        def first_of(parts):
            g0 = left_of(tab, 0, 0, parts[0])
            g1 = left_of(tab, 0, 1, parts[1])
            top, bot = g0 + g1, g0 - g1
            xr = jnp.concatenate([top[:HALF], bot[:HALF]], axis=0)
            xi = jnp.concatenate([top[HALF:], bot[HALF:]], axis=0)
            a0 = jnp.concatenate([xr[:, :HALF], xi[:, :HALF]], axis=1)
            a1 = jnp.concatenate([xr[:, HALF:], xi[:, HALF:]], axis=1)
            return split(a0), split(a1)

        def back_of(j, parts):
            b0 = right_of(parts[0], tab, 1, 0)
            b1 = right_of(parts[1], tab, 1, 1)
            lo, hi = b0 + b1, b0 - b1
            br = jnp.concatenate([lo[:, :HALF], hi[:, :HALF]], axis=1)
            bi = jnp.concatenate([lo[:, HALF:], hi[:, HALF:]], axis=1)
            far[m * NPAT + j, 0] = br
            far[m * NPAT + j, 1] = bi
            pr, pi = window_of(j)
            real, imag = pr * br + pi * bi, pr * bi - pi * br
            numer[0, m] = real if j == 0 else numer[0, m] + real
            numer[1, m] = imag if j == 0 else numer[1, m] + imag

        fixed = [fixed_of(j) for j in positions]
        halfway = [first_of(parts) for parts in fixed]
        for j, parts in zip(positions, halfway):
            back_of(j, parts)

    line_rows = pl.ds(pl.multiple_of(me.v * 64, 64), 64)
    core_sems, line_sems, plane_sems = (core_send, core_recv), (line_send, line_recv), (plane_send, plane_recv)
    back_plane_sems, back_line_sems = (back_plane_send, back_plane_recv), (back_line_send, back_line_recv)
    back_core_sems, edge_sems = (back_core_send, back_core_recv), (edge_send, edge_recv)

    def mine(m):
        return denom[...] if m == MODES else numer[me.core, m]

    def core_start(m):
        send(denom if m == MODES else numer.at[1 - me.core, m], from_core.at[m], core_sems, m, me.sibling())

    def line_start(m):
        await_bytes(from_core.at[m], core_recv.at[m])
        part[m] = mine(m) + from_core[m]
        for k in range(1, 4):
            device, there = me.on_line(k)
            source = part.at[m, pl.ds(pl.multiple_of(there * 64, 64), 64), :]
            send(source, from_line.at[m, k - 1], line_sems, m, device)

    def plane_start(m):
        await_bytes(from_line.at[m], line_recv.at[m])
        total = part[m, line_rows, :] + from_line[m, 0] + from_line[m, 1] + from_line[m, 2]
        for k in range(16):
            block[m, k] = total[(k // 2) * 8:(k // 2) * 8 + 8, (k % 2) * HALF:(k % 2 + 1) * HALF]

        for k in range(1, 16):
            device, there = me.in_plane(k)
            send(block.at[m, there], from_plane.at[m, k - 1], plane_sems, m, device)

    def total_of(m):
        await_bytes(from_plane.at[m], plane_recv.at[m])
        total = block[m, me.number]
        for k in range(15):
            total = total + from_plane[m, k]
        return total

    def denom_end():
        scale[...] = total_of(MODES) + 1.0

    def back_start(m):
        row = pl.multiple_of(me.v * 64 + (me.number // 2) * 8, 8)
        column = pl.multiple_of(lax.rem(me.number, 2) * HALF, HALF)
        old = probe[me.core, m, pl.ds(row, 8), pl.ds(column, HALF)]
        tiles[m, me.number] = (old + total_of(m)) / scale[...]
        own = tiles.at[m, me.number]

        for k in range(1, 16):
            send(own, own, back_plane_sems, m, me.in_plane(k)[0])

    def back_line_start(m):
        await_bytes(tiles.at[m, pl.ds(0, 15)], back_plane_recv.at[m])
        rows = [jnp.concatenate([tiles[m, 2 * i], tiles[m, 2 * i + 1]], axis=1) for i in range(8)]
        fresh[me.core, m, line_rows, :] = jnp.concatenate(rows, axis=0)
        own = fresh.at[me.core, m, line_rows, :]
        for k in range(1, 4):
            send(own, own, back_line_sems, m, me.on_line(k)[0])

    def back_core_start(m):
        await_bytes(fresh.at[me.core, m, pl.ds(0, 192), :], back_line_recv.at[m])
        send(fresh.at[me.core, m], fresh.at[me.core, m], back_core_sems, m, me.sibling())

    def back_end(m):
        await_bytes(fresh.at[1 - me.core, m], back_core_recv.at[m])
        for plane in range(2):
            probe_out[plane, m] = fresh[plane, m]

    def spread_plane(plane, j, block):
        rows = pl.ds(pl.multiple_of(j * PAT, PAT), PAT)
        by = jnp.broadcast_to(work[pl.ds(POWER + NPAT + j, 1), PAT:], (PAT, PAT)).astype(jnp.int32)
        by = jnp.concatenate([by, by], axis=1)
        columns = jnp.where(along((PAT, TILE), 1) - along((PAT, TILE), 0) == by, 1.0, 0.0).astype(BF16)
        h, l = split(block)
        h, l = split(dot(h, columns) + dot(l, columns))
        spread_hi[plane, rows, :] = h
        spread_lo[plane, rows, :] = l

    def spread(first, last):
        def one(j, _):
            real, imag = jnp.zeros((PAT, PAT), F32), jnp.zeros((PAT, PAT), F32)
            for m in range(MODES):
                br, bi, qr, qi = far[m * NPAT + j, 0], far[m * NPAT + j, 1], probe[0, m], probe[1, m]
                real = real + qr * br + qi * bi
                imag = imag + qr * bi - qi * br
            spread_plane(0, j, real)
            spread_plane(1, j, imag)
            return 0

        lax.fori_loop(first, last, one, 0, unroll=True)

    def spread_weights():
        power = sum(probe[0, m] * probe[0, m] + probe[1, m] * probe[1, m] for m in range(MODES))
        for j in range(NPAT):
            spread_plane(2, j, power)

    def update(starts, count):
        chosen = []
        for j in range(NPAT):
            by = jnp.broadcast_to(work[POWER + j:POWER + j + 1, PAT:], (count, PAT)).astype(jnp.int32)
            away = along((count, PAT), 0) - along((count, PAT), 1)
            chosen.append(jnp.concatenate([jnp.where(away + start == by, 1.0, 0.0).astype(BF16) for start in starts], axis=0))
        chosen = jnp.concatenate(chosen, axis=1)
        sums = [dot(chosen, spread_hi[plane]) + dot(chosen, spread_lo[plane]) for plane in range(3)]
        for i, start in enumerate(starts):
            rows, here = slice(start, start + count), slice(i * count, (i + 1) * count)
            inverse_weight = 1.0 / (sums[2][here] + 1.0)
            for plane in range(2):
                mid[plane, rows, :] = (obj[plane, rows, :] + sums[plane][here]) * inverse_weight

    def dual(side, plane):
        start = DUALS + (2 * side + plane) * EDGE
        return work[start:start + EDGE, :]

    def mask_start():
        wide = lambda ref, i: jnp.broadcast_to(ref[0:1, i:i + 1], (1, TILE))
        number = along((1, TILE), 1) // BLOCK
        first, second, count = wide(pieces, 0) == number, wide(pieces, 1) == number, wide(live, 0)
        last = jnp.broadcast_to(me.region, (1, TILE)) >= 31
        flag = lambda chosen: jnp.where(chosen, 1.0, 0.0).astype(F32)
        active = flag(first & (count > 0)) + flag(second & (count > 1))
        mask[0:1, :] = flag(first)
        mask[1:2, :] = flag(second)
        mask[2:3, :] = jnp.where(last, 0.0, active)
        mask[3:8, :] = jnp.zeros((5, TILE), F32)
        send(mask, mask_in, edge_sems, 0, me.region_by(1))

    def edge_start():
        await_bytes(mask_in, edge_recv.at[0])
        for plane in range(2):
            up[plane] = mid[plane, :EDGE] + dual(0, plane)
            low[plane] = mid[plane, TILE - EDGE:] + dual(1, plane)
            up_sent[plane] = packed(up[plane], mask_in)
            low_sent[plane] = packed(low[plane], mask)

    def edge_send_plane(plane):
        send(up_sent.at[plane], from_below.at[plane], edge_sems, 1 + plane, me.region_by(-1))
        send(low_sent.at[plane], from_above.at[plane], edge_sems, 3 + plane, me.region_by(1))

    def edge_end():
        for plane in range(2):
            await_bytes(from_below.at[plane], edge_recv.at[1 + plane])
            await_bytes(from_above.at[plane], edge_recv.at[3 + plane])
            here = mid[plane, TILE - EDGE:]
            agreed = 0.5 * (low[plane] + unpacked(from_below[plane], mask))
            active = jnp.broadcast_to(mask[2:3, :], (EDGE, TILE)) > 0.5
            bottom_out[plane] = jnp.where(active, dual(1, plane) + (here - agreed), dual(1, plane))
            mid[plane, TILE - EDGE:] = jnp.where(active, agreed, here)
            here = mid[plane, :EDGE]
            agreed = 0.5 * (unpacked(from_above[plane], mask_in) + up[plane])
            active = jnp.broadcast_to(mask_in[2:3, :], (EDGE, TILE)) > 0.5
            top_out[plane] = jnp.where(active, dual(0, plane) + (here - agreed), dual(0, plane))
            mid[plane, :EDGE] = jnp.where(active, agreed, here)

    wait_loads(0, 10)
    wait_loads(15, 16)
    forward(0)
    wait_loads(10, 15)
    wait_loads(16, 19)
    denom[...] = work[POWER:POWER + PAT, :PAT]
    forward(1)
    forward(2)
    pl.semaphore_wait(barrier, 21)
    mask_start()
    core_start(MODES)
    forward(3)
    line_start(MODES)
    inverse(0, 0, 4)
    core_start(0)
    inverse(1, 0, 2)
    line_start(0)
    inverse(1, 2, 4)
    core_start(1)
    plane_start(MODES)
    inverse(2, 0, 2)
    line_start(1)
    inverse(2, 2, 4)
    core_start(2)
    inverse(3, 0, 2)
    plane_start(0)
    line_start(2)
    inverse(3, 2, 4)
    core_start(3)
    spread(0, 1)
    line_start(3)
    plane_start(1)
    denom_end()
    spread(1, 2)
    spread(2, 4)
    back_start(0)
    plane_start(2)
    spread_weights()
    wait_loads(19, LOADS)
    update((0, TILE - EDGE), EDGE)
    edge_start()
    plane_start(3)
    back_start(1)
    back_line_start(0)
    update((EDGE,), TILE // 2 - EDGE)
    back_start(2)
    back_start(3)
    update((TILE // 2,), TILE // 2 - EDGE)
    back_line_start(1)
    edge_send_plane(0)
    back_line_start(2)
    edge_send_plane(1)
    back_core_start(0)
    back_line_start(3)
    back_core_start(1)
    back_core_start(2)
    back_end(0)
    back_core_start(3)
    back_end(1)
    back_end(2)
    edge_end()
    back_end(3)

    for m in range(SUMS):
        await_bytes(from_core.at[m], core_send.at[m])
        await_bytes(from_line.at[m], line_send.at[m])
        await_bytes(from_plane.at[m], plane_send.at[m])
    for m in range(MODES):
        await_bytes(tiles.at[m, pl.ds(0, 15)], back_plane_send.at[m])
        await_bytes(fresh.at[0, m, pl.ds(0, 192), :], back_line_send.at[m])
        await_bytes(fresh.at[0, m], back_core_send.at[m])
    await_bytes(mask_in, edge_send.at[0])
    for plane in range(2):
        await_bytes(up_sent.at[plane], edge_send.at[1 + plane])
        await_bytes(low_sent.at[plane], edge_send.at[3 + plane])


def write_out(mid, probe, top, bottom, mid_out, probe_out, top_out, bottom_out, sems):
    copies = []
    for plane in range(2):
        copies.append((top.at[plane], top_out.at[plane]))
        copies.append((bottom.at[plane], bottom_out.at[plane]))
        for i in range(2):
            rows = pl.ds(i * PAT, PAT)
            copies.append((mid.at[plane, rows], mid_out.at[plane, rows]))
            copies.append((probe.at[plane, pl.ds(2 * i, 2)], probe_out.at[plane, pl.ds(2 * i, 2)]))
    copies = [pltpu.make_async_copy(source, target, sems.at[i]) for i, (source, target) in enumerate(copies)]
    for copy in copies:
        copy.start()
    for copy in copies:
        copy.wait()


def local(object_field, probe, amplitudes, positions, dual_top, dual_bottom, pieces, live):
    tab = tables()
    vmem = pl.BlockSpec(memory_space=pltpu.VMEM)
    smem = pl.BlockSpec(memory_space=pltpu.SMEM)
    far = pl.BlockSpec(memory_space=pltpu.HBM)
    anywhere = pl.BlockSpec(memory_space=pl.ANY)
    buf = lambda *shape: pltpu.VMEM(shape, F32)
    half = lambda *shape: pltpu.VMEM(shape, BF16)
    dma = lambda *shape: pltpu.SemaphoreType.DMA(shape)
    edge, sent = (2, EDGE, TILE), (2, EDGE, KP * BLOCK)
    shape = lambda *dims: jax.ShapeDtypeStruct(dims, F32)
    prepared = pl.pallas_call(
        prepare,
        out_shape=shape(DUALS + PAT, TILE),
        in_specs=[smem] + [far] * 3,
        out_specs=far,
        scratch_shapes=[buf(DUALS + PAT, TILE), buf(2, TILE, TILE), dma(14)],
        compiler_params=pltpu.CompilerParams(vmem_limit_bytes=60 * 1024 * 1024),
    )(positions.T, object_field, dual_top, dual_bottom)
    results = pl.pallas_call(
        kernel,
        out_shape=(shape(2, TILE, TILE), shape(2, MODES, PAT, PAT), shape(*edge), shape(*edge)),
        in_specs=[far] * 3 + [vmem] * 2 + [far] * 2,
        out_specs=(vmem,) * 4,
        scratch_shapes=[
            buf(MODES * NPAT, 2, PAT, PAT), buf(NPAT, 2, PAT, PAT),
            half(3, NPAT * PAT, TILE), half(3, NPAT * PAT, TILE), buf(2, MODES, PAT, PAT),
            buf(SUMS, PAT, PAT), buf(SUMS, PAT, PAT), buf(SUMS, 3, 64, PAT), buf(SUMS, 16, 8, HALF), buf(SUMS, 15, 8, HALF),
            buf(MODES, 16, 8, HALF), buf(2, MODES, PAT, PAT), buf(8, HALF),
            buf(DUALS + PAT, TILE), buf(PAT, PAT), buf(2, MODES, PAT, PAT), half(2, 2, 2, PAT, PAT), buf(2, TILE, TILE), buf(NPAT, PAT, PAT), half(2, PAT, PAT), buf(8, TILE), buf(8, TILE), buf(*edge), buf(*edge), buf(*sent), buf(*sent), buf(*sent), buf(*sent),
        ] + [dma(SUMS)] * 6 + [dma(MODES)] * 6 + [dma(5), dma(5), dma(LOADS)],
        compiler_params=pltpu.CompilerParams(vmem_limit_bytes=LIMIT * 1024 * 1024, collective_id=0, has_side_effects=True),
    )(prepared, probe, jnp.asarray(tab), pieces.T, live, object_field, amplitudes)
    return pl.pallas_call(
        write_out,
        out_shape=(shape(2, TILE, TILE), shape(2, MODES, PAT, PAT), shape(*edge), shape(*edge)),
        in_specs=[anywhere] * 4,
        out_specs=(far,) * 4,
        scratch_shapes=[dma(12)],
        compiler_params=pltpu.CompilerParams(vmem_limit_bytes=1024 * 1024),
    )(*results)


def solution(mesh):
    tiles = P(None, "region", "group")
    return jax.shard_map(
        local,
        mesh=mesh,
        in_specs=(tiles, P(), P("region", "group", None), P("region", "group"), tiles, tiles, P("region", "group"), P("region", "group")),
        out_specs=(tiles, P(), tiles, tiles),
        check_vma=False,
    )
```
